512 devices in a mesh: tm: 16 (over y, core), height: 8 (over z), width: 4 (over x).
Axes of the slice: x: 4, y: 8, z: 8, core: 2. Of those that a mesh axis runs over, the one named last changes fastest.
Arguments:
- latents: bfloat16 [64, 64, 32, 512], P('tm', 'height', 'width'), may hold values from -6 to 6
- spatial_taps: float32 [3, 3, 512], replicated, may hold values from -2 to 2
- kernel_taps: bfloat16 [64, 512], replicated, may hold values from -0.4 to 0.4
- skip_gain: float32 [512], replicated, may hold values from 0.5 to 1.5
- gate_weight: bfloat16 [512, 512], replicated, may hold values from -0.25 to 0.25
- value_weight: bfloat16 [512, 512], replicated, may hold values from -0.25 to 0.25
- out_weight: bfloat16 [512, 512], replicated, may hold values from -0.25 to 0.25
Outputs:
- mixed_out: bfloat16 [64, 64, 32, 512], P('tm', 'height', 'width')
The draws below stay inside these ranges and needn't reach their ends.
All inputs are finite; a program needn't handle non-finite values.
Results may differ from the reference program's by a relative error of at most 0.0064.
Values may be sent and summed in bfloat16 or wider, within the bound.
A program may use at most 64 MiB of HBM per device.

```python
import math
import jax
import jax.numpy as jnp
from jax import lax

FEATURE_WIDTH = 512
F_DEV = 4
MOVIE_LENGTH = 64
H = 64
W = 32
N_TM = 16


def draw_kernel_taps(key, part):
    key = jax.random.fold_in(key, 11)
    keys = jax.random.split(key, 6)
    lagging_images = jnp.arange(MOVIE_LENGTH, dtype=jnp.float32)[:, None]
    low = math.log(30.0)
    high = math.log(4.0 * MOVIE_LENGTH)
    support_radius = jnp.exp(jax.random.uniform(keys[0], (1, FEATURE_WIDTH), jnp.float32, low, high))
    jump_increment = jax.random.uniform(keys[1], (1, FEATURE_WIDTH), jnp.float32, 0.0, 0.3)
    cycle_shift = jax.random.uniform(keys[2], (1, FEATURE_WIDTH), jnp.float32, -math.pi, math.pi)
    rough_guess = jax.random.uniform(keys[3], (MOVIE_LENGTH, FEATURE_WIDTH), jnp.float32, 0.5, 1.5)
    pixel_locations = jax.random.randint(keys[4], (3,), 1, MOVIE_LENGTH).astype(jnp.float32)
    discarded_entries = jax.random.uniform(keys[5], (3, FEATURE_WIDTH), jnp.float32, 0.5, 0.8)
    packet_bundles = jnp.ones((MOVIE_LENGTH, FEATURE_WIDTH), jnp.float32)
    for chosen_position in range(3):
        packet_bundles = packet_bundles * jnp.where(lagging_images >= pixel_locations[chosen_position], discarded_entries[chosen_position][None, :], 1.0)
    magnitude_multiplier = jnp.sqrt(2.0 / support_radius)
    response_weights = magnitude_multiplier * jnp.exp(-lagging_images / support_radius) * jnp.cos(jump_increment * lagging_images + cycle_shift) * rough_guess * packet_bundles
    return jnp.clip(response_weights, -0.3984375, 0.3984375).astype(jnp.bfloat16)


def levels(stream_key, shape, pieces, low, largest):
    def one(dim, blocks):
        steps = jax.random.uniform(jax.random.fold_in(jax.random.fold_in(stream_key, 6), dim), (blocks,), jnp.float32, low / len(pieces), largest / len(pieces))
        return jnp.repeat(jnp.exp(steps), shape[dim] // blocks).reshape((-1,) + (1,) * (len(shape) - dim - 1))

    gain = one(*pieces[0])
    for cut in pieces[1:]:
        gain = gain * one(*cut)
    return gain


def centred(rng, extent, deviation, most, cuts=(), kind=jnp.bfloat16):
    loudness = levels(rng, extent, cuts, -0.22, 0.18) if cuts else 1.0
    values = jax.random.normal(rng, extent, jnp.float32) * deviation * loudness
    return jnp.minimum(jnp.maximum(values, -most), most).astype(kind)


def setup_inputs(seed: int = 0) -> dict:
    splits = jax.random.split(jax.random.key(seed), 8)
    latents = centred(splits[0], (MOVIE_LENGTH, H, W, FEATURE_WIDTH), 1.0, 6.0, ((0, 16), (1, 8), (2, 4)))
    spatial_taps = centred(splits[1], (3, 3, FEATURE_WIDTH), 9 ** -0.5, 2.0, (), jnp.float32)
    kernel_taps = draw_kernel_taps(jax.random.fold_in(splits[7], 71), 0)
    skip_gain = jnp.clip(jax.random.uniform(splits[3], (FEATURE_WIDTH,), jnp.float32, 0.5, 1.5), 0.5, 1.5)
    gate_weight = centred(splits[4], (FEATURE_WIDTH, FEATURE_WIDTH), FEATURE_WIDTH ** -0.5, 0.25)
    value_weight = centred(splits[5], (FEATURE_WIDTH, FEATURE_WIDTH), FEATURE_WIDTH ** -0.5, 0.25)
    out_weight = centred(splits[6], (FEATURE_WIDTH, FEATURE_WIDTH), FEATURE_WIDTH ** -0.5, 0.25)
    return {"latents": latents, "spatial_taps": spatial_taps, "kernel_taps": kernel_taps, "skip_gain": skip_gain, "gate_weight": gate_weight, "value_weight": value_weight, "out_weight": out_weight}


def spatial_mix(padded, spatial_taps):
    rows = padded.shape[1] - 2
    cols = padded.shape[2] - 2
    total = jnp.zeros((padded.shape[0], rows, cols, padded.shape[3]), jnp.float32)
    for first in range(3):
        for second in range(3):
            window = padded[:, first:first + rows, second:second + cols, :].astype(jnp.float32)
            total = total + window * spatial_taps[first, second]
    return total.astype(jnp.bfloat16)


def reference(latents, spatial_taps, kernel_taps, skip_gain, gate_weight, value_weight, out_weight):
    frames, rows, cols, chans = latents.shape
    blocks = latents.reshape(N_TM, F_DEV, rows, cols, chans)

    def filter_block(block):
        padded = jnp.pad(block, ((0, 0), (1, 1), (1, 1), (0, 0)))
        return spatial_mix(padded, spatial_taps)

    spatial = lax.map(filter_block, blocks).reshape(frames, rows, cols, chans)
    groups = chans // 32
    lag = jnp.arange(frames, dtype=jnp.int32)[:, None] - jnp.arange(frames, dtype=jnp.int32)[None, :]
    index = jnp.clip(lag, 0, frames - 1).astype(jnp.int32)
    columns = spatial.reshape(frames, rows * cols, groups, 32).transpose(2, 0, 1, 3)
    grouped_taps = kernel_taps.reshape(frames, groups, 32).transpose(1, 2, 0)

    def convolve(inputs):
        column_block, tap_block = inputs
        toeplitz = jnp.where(lag[None, :, :] >= 0, jnp.take(tap_block, index, axis=1).astype(jnp.float32), jnp.float32(0.0))
        return jnp.einsum("cts,sxc->txc", toeplitz, column_block.astype(jnp.float32), precision=lax.Precision.HIGHEST)

    causal = lax.map(convolve, (columns, grouped_taps))
    causal = causal.transpose(1, 2, 0, 3).reshape(frames, rows, cols, chans)
    mixed = (causal + skip_gain * spatial.astype(jnp.float32)).astype(jnp.bfloat16)

    def project(inputs):
        frame_in, frame_mixed = inputs
        flat_in = frame_in.reshape(rows * cols, chans)
        flat_mixed = frame_mixed.reshape(rows * cols, chans)
        gate = jax.nn.silu(jnp.dot(flat_in, gate_weight, preferred_element_type=jnp.float32))
        value = jnp.dot(flat_mixed, value_weight, preferred_element_type=jnp.float32)
        hidden = (value * gate).astype(jnp.bfloat16)
        result = jnp.dot(hidden, out_weight, preferred_element_type=jnp.float32).astype(jnp.bfloat16)
        return result.reshape(rows, cols, chans)

    return lax.map(project, (latents, mixed))
```

```python
import functools

import jax
import jax.numpy as jnp
from jax import lax
from jax.experimental import pallas as pl
from jax.experimental.pallas import tpu as pltpu
from jax.sharding import PartitionSpec as P

MESH = pl.DeviceIdType.MESH
F32 = jnp.float32
BF16 = jnp.bfloat16
ORDER = (1, 7, 2, 6, 3, 5, 4, 0)
AROUND = ((-1, 0), (1, 0), (0, -1), (0, 1), (-1, -1), (-1, 1), (1, -1), (1, 1))


def owner(group, tile):
    return ((group % 2) * 4 + tile) * 2 + group // 2


def kernel(
    lat, taps, ktaps, skip, wg, wv, hid,
    xl, tv, kt, kf, kb, sk, wgv, wvv, s0, s1, colb, crnb, hrow, hcol, hcrn, hc32, hk32,
    sendb, xin, retb, mixin, gate,
    lsem, hs, hr, fs, fr, rs, rr,
):
    me = lax.axis_index("tm")
    ring, core = me // 2, lax.rem(me, 2)
    hi, wi = lax.axis_index("height"), lax.axis_index("width")
    nh, nw = lax.axis_size("height"), lax.axis_size("width")
    mine = lax.rem(ring, 4)
    lanes = pl.ds(pl.multiple_of(mine * 128, 128), 128)

    loads = [
        pltpu.make_async_copy(lat, xl, lsem.at[0]),
        pltpu.make_async_copy(taps, tv, lsem.at[1]),
        pltpu.make_async_copy(ktaps.at[:, lanes], kt, lsem.at[2]),
        pltpu.make_async_copy(skip.at[:, lanes], sk, lsem.at[3]),
        pltpu.make_async_copy(wg, wgv, lsem.at[4]),
        pltpu.make_async_copy(wv, wvv, lsem.at[5]),
    ]
    loads[0].start()
    loads[1].start()

    def peer(index):
        return (index, hi, wi)

    def beside(step):
        dh, dw = step
        return (me, lax.rem(hi + dh + nh, nh), lax.rem(wi + dw + nw, nw))

    barrier = pltpu.get_barrier_semaphore()
    for step in range(1, 16):
        pl.semaphore_signal(barrier, inc=1, device_id=peer(lax.rem(me + step, 16)), device_id_type=MESH)
    for step in AROUND:
        pl.semaphore_signal(barrier, inc=1, device_id=beside(step), device_id_type=MESH)
    for load in loads[2:]:
        load.start()

    loads[0].wait()
    for tile in range(4):
        for frame in range(4):
            at = (tile * 4 + frame) * 64
            s0[at : at + 64] = xl[frame, :, :, tile * 128 : tile * 128 + 128].astype(F32).reshape(64, 128)
    colb[0] = s0[pl.ds(0, 128, stride=8)].astype(BF16)
    colb[1] = s0[pl.ds(7, 128, stride=8)].astype(BF16)
    for n, site in enumerate((0, 7, 56, 63)):
        crnb[n] = s0[pl.ds(site, 16, stride=64)].astype(BF16)

    pl.semaphore_wait(barrier, 23)

    pieces = (
        (xl.at[:, 0], hrow.at[1]),
        (xl.at[:, 7], hrow.at[0]),
        (colb.at[0], hcol.at[1]),
        (colb.at[1], hcol.at[0]),
        (crnb.at[0], hcrn.at[3]),
        (crnb.at[1], hcrn.at[2]),
        (crnb.at[2], hcrn.at[1]),
        (crnb.at[3], hcrn.at[0]),
    )
    opposite = (1, 0, 3, 2, 7, 6, 5, 4)
    halo = []
    for n, (src, dst) in enumerate(pieces):
        halo.append(
            pltpu.make_async_remote_copy(
                src_ref=src, dst_ref=dst, send_sem=hs.at[n], recv_sem=hr.at[opposite[n]],
                device_id=beside(AROUND[n]), device_id_type=MESH,
            )
        )
    for copy in halo:
        copy.start()

    sub = lax.broadcasted_iota(jnp.int32, (8, 128), 0)
    first, last = sub == 0, sub == 7
    edge = first | last

    def tap(tile, a, b):
        return tv[a, pl.ds(b, 1), pl.ds(pl.multiple_of(tile * 128, 128), 128)]

    def west(x):
        return jnp.where(first, 0.0, pltpu.roll(x, 1, 0))

    def east(x):
        return jnp.where(last, 0.0, pltpu.roll(x, 7, 0))

    loads[1].wait()

    def inside(i, carry):
        tile, frame = i // 4, lax.rem(i, 4)
        base = pl.multiple_of(i * 64, 64)
        weights = [[tap(tile, a, b) for b in range(3)] for a in range(3)]
        total = [None] * 8
        for r in range(8):
            x = s0[pl.ds(base + r * 8, 8)]
            moved = (west(x), x, east(x))
            for a in range(3):
                o = r + 1 - a
                if 0 <= o < 8:
                    part = weights[a][0] * moved[0] + weights[a][1] * moved[1] + weights[a][2] * moved[2]
                    total[o] = part if total[o] is None else total[o] + part
        for r in (0, 5, 6, 7):
            s1[pl.ds(base + r * 8, 8)] = total[r]
        for r in (1, 2, 3, 4):
            s1[pl.ds(base + r * 8, 8)] = total[r]
        mixed = [
            jnp.where(edge, pltpu.roll(total[5], 6, 0), total[1]),
            jnp.where(edge, pltpu.roll(total[5], 4, 0), total[2]),
            jnp.where(edge, pltpu.roll(total[5], 2, 0), total[3]),
            jnp.where(edge, pltpu.roll(total[6], 6, 0), total[4]),
        ]
        sendb[tile * 2, frame] = jnp.concatenate(mixed[:2], 0).astype(BF16)
        sendb[(4 + tile) * 2, frame] = jnp.concatenate(mixed[2:], 0).astype(BF16)
        return carry

    lax.fori_loop(0, 16, inside, 0)

    def forward(dest):
        return pltpu.make_async_remote_copy(
            src_ref=sendb.at[dest], dst_ref=xin.at[me], send_sem=fs.at[dest], recv_sem=fr.at[me],
            device_id=peer(dest), device_id_type=MESH,
        )

    def keep():
        return pltpu.make_async_copy(sendb.at[me], xin.at[me], fr.at[me])

    def spread(which):
        for step in ORDER:
            dest = lax.rem(ring + step, 8) * 2 + which
            if step:
                forward(dest).start()
            else:
                @pl.when(core == which)
                def _():
                    keep().start()

                @pl.when(core != which)
                def _():
                    forward(dest).start()

    spread(0)

    for n, (src, dst) in enumerate(pieces):
        pltpu.make_async_remote_copy(
            src_ref=src, dst_ref=(hrow.at[0], hrow.at[1], hcol.at[0], hcol.at[1], hcrn.at[0], hcrn.at[1], hcrn.at[2], hcrn.at[3])[n],
            send_sem=hs.at[n], recv_sem=hr.at[n], device_id=beside(AROUND[n]), device_id_type=MESH,
        ).wait_recv()

    up = (hi > 0).astype(F32)
    down = (hi < nh - 1).astype(F32)
    left = (wi > 0).astype(F32)
    right = (wi < nw - 1).astype(F32)
    hk32[0] = hcol[0].astype(F32) * left
    hk32[1] = hcol[1].astype(F32) * right
    hc32[0] = hcrn[0].astype(F32) * (up * left)
    hc32[1] = hcrn[1].astype(F32) * (up * right)
    hc32[2] = hcrn[2].astype(F32) * (down * left)
    hc32[3] = hcrn[3].astype(F32) * (down * right)

    def border(i, carry):
        tile, frame = i // 4, lax.rem(i, 4)
        base = pl.multiple_of(i * 64, 64)
        chans = pl.ds(pl.multiple_of(tile * 128, 128), 128)
        weights = [[tap(tile, a, b) for b in range(3)] for a in range(3)]
        above = hrow[0, frame, :, chans].astype(F32) * up
        below = hrow[1, frame, :, chans].astype(F32) * down
        row0 = s1[pl.ds(base, 8)] + (weights[0][0] * west(above) + weights[0][1] * above + weights[0][2] * east(above))
        row7 = s1[pl.ds(base + 56, 8)] + (weights[2][0] * west(below) + weights[2][1] * below + weights[2][2] * east(below))
        row6 = s1[pl.ds(base + 48, 8)]
        s1[pl.ds(base, 8)] = row0
        s1[pl.ds(base + 56, 8)] = row7
        ends = [
            jnp.where(edge, pltpu.roll(row6, 4, 0), row0),
            jnp.where(edge, pltpu.roll(row6, 2, 0), row7),
        ]
        sides = []
        for n, c in ((0, 0), (1, 7)):
            own = s1[pl.ds(base + c, 8, stride=8)]
            out = hk32[n, pl.ds(pl.multiple_of(i * 8, 8), 8)]
            over = jnp.where(first, hc32[n, pl.ds(i, 1)], pltpu.roll(out, 1, 0))
            under = jnp.where(last, hc32[2 + n, pl.ds(i, 1)], pltpu.roll(out, 7, 0))
            b = 2 * n
            sides.append(own + (weights[0][b] * over + weights[1][b] * out + weights[2][b] * under))
        sendb[tile * 2 + 1, frame] = jnp.concatenate(sides, 0).astype(BF16)
        sendb[(4 + tile) * 2 + 1, frame] = jnp.concatenate(ends, 0).astype(BF16)
        return carry

    lax.fori_loop(0, 16, border, 0)
    spread(1)

    loads[2].wait()
    loads[3].wait()
    kf[...] = kt[...].astype(F32)
    kb[0:8] = jnp.zeros((8, 8, 128), F32)

    def widen(lag, carry):
        kb[8 + lag] = jnp.broadcast_to(kf[pl.ds(lag, 1)], (8, 128))
        return carry

    lax.fori_loop(0, 64, widen, 0)
    kb[8] = kb[8] + jnp.broadcast_to(sk[...], (8, 128))
    loads[4].wait()
    raw = jnp.dot(xl[...].reshape(256, 512), wgv[...], preferred_element_type=F32)
    gate[...] = raw / (1.0 + jnp.exp(-raw))
    loads[5].wait()

    keep().wait()
    for step in range(1, 16):
        src = lax.rem(me + step, 16)
        pltpu.make_async_remote_copy(
            src_ref=sendb.at[src], dst_ref=xin.at[src], send_sem=fs.at[src], recv_sem=fr.at[src],
            device_id=peer(src), device_id_type=MESH,
        ).wait_recv()

    def back(dest):
        return pltpu.make_async_remote_copy(
            src_ref=retb.at[dest], dst_ref=mixin.at[me], send_sem=rs.at[dest], recv_sem=rr.at[me],
            device_id=peer(dest), device_id_type=MESH,
        )

    def own():
        return pltpu.make_async_copy(retb.at[me], mixin.at[me], rr.at[me])

    for step in ORDER:
        chip = lax.rem(ring + step, 8)

        def lagged(source, acc):
            shift = 8 + 8 * (chip - source)
            for s in range(8):
                x = xin[source * 2 + s // 4, s % 4].astype(F32).reshape(1, 2, 8, 128)
                acc = acc + kb[pl.ds(shift - s, 8)].reshape(8, 1, 8, 128) * x
            return acc

        acc = lax.fori_loop(0, chip + 1, lagged, jnp.zeros((8, 2, 8, 128), F32))
        retb[pl.ds(chip * 2, 2)] = acc.reshape(2, 4, 16, 128).astype(BF16)
        if step:
            back(chip * 2).start()
            back(chip * 2 + 1).start()
        else:
            own().start()
            back(chip * 2 + 1 - core).start()

    def arrived(which):
        for step in ORDER:
            src = lax.rem(ring + step, 8) * 2 + which

            def wait():
                pltpu.make_async_remote_copy(
                    src_ref=retb.at[src], dst_ref=mixin.at[src], send_sem=rs.at[src], recv_sem=rr.at[src],
                    device_id=peer(src), device_id_type=MESH,
                ).wait_recv()

            if step:
                wait()
            else:
                pl.when(core == which)(lambda: own().wait())
                pl.when(core != which)(wait)

    def values(which):
        rows = []
        for group in (2 * which, 2 * which + 1):
            rows.append(jnp.concatenate([mixin[owner(group, t)].reshape(64, 128) for t in range(4)], 1))
        return jnp.dot(jnp.concatenate(rows, 0), wvv[...], preferred_element_type=F32)

    def part(block, group, tile, frame, half):
        at = group * 64 + frame * 16 + half * 8
        return block[at : at + 8, tile * 128 : tile * 128 + 128]

    arrived(0)
    v = values(0)
    for tile in range(4):
        for frame in range(4):
            base = (tile * 4 + frame) * 64
            one, two = part(v, 0, tile, frame, 0), part(v, 0, tile, frame, 1)
            three, four = part(v, 1, tile, frame, 0), part(v, 1, tile, frame, 1)
            s1[base + 8 : base + 16] = one
            s1[base + 16 : base + 24] = two
            s1[base + 24 : base + 32] = three
            s1[base + 32 : base + 40] = four
            s1[base + 40 : base + 48] = jnp.where(
                sub < 3, pltpu.roll(one, 2, 0), jnp.where(sub < 5, pltpu.roll(two, 4, 0), pltpu.roll(three, 6, 0))
            )
            s1[base + 48 : base + 56] = pltpu.roll(four, 2, 0)
    arrived(1)
    v = values(1)
    for tile in range(4):
        for frame in range(4):
            base = (tile * 4 + frame) * 64
            top, bottom = part(v, 1, tile, frame, 0), part(v, 1, tile, frame, 1)
            s1[base : base + 8] = top
            s1[base + 56 : base + 64] = bottom
            s1[base + 48 : base + 56] = jnp.where(
                sub < 3, s1[base + 48 : base + 56], jnp.where(sub < 5, pltpu.roll(top, 4, 0), pltpu.roll(bottom, 6, 0))
            )
            s1[pl.ds(base, 8, stride=8)] = part(v, 0, tile, frame, 0)
            s1[pl.ds(base + 7, 8, stride=8)] = part(v, 0, tile, frame, 1)
            rows, chans = slice(frame * 64, frame * 64 + 64), slice(tile * 128, tile * 128 + 128)
            hid[rows, chans] = (s1[base : base + 64] * gate[rows, chans]).astype(BF16)

    for copy in halo:
        copy.wait_send()
    for step in range(1, 16):
        dest = lax.rem(me + step, 16)
        forward(dest).wait_send()
        back(dest).wait_send()


def body(latents, spatial_taps, kernel_taps, skip_gain, gate_weight, value_weight, out_weight):
    dma = pltpu.SemaphoreType.DMA
    hidden = pl.pallas_call(
        kernel,
        out_shape=jax.ShapeDtypeStruct((256, 512), BF16),
        in_specs=[pl.BlockSpec(memory_space=pl.ANY)] * 6,
        out_specs=pl.BlockSpec(memory_space=pltpu.VMEM),
        scratch_shapes=[
            pltpu.VMEM((4, 8, 8, 512), BF16),
            pltpu.VMEM((3, 3, 512), F32),
            pltpu.VMEM((64, 128), BF16),
            pltpu.VMEM((64, 128), F32),
            pltpu.VMEM((72, 8, 128), F32),
            pltpu.VMEM((1, 128), F32),
            pltpu.VMEM((512, 512), BF16),
            pltpu.VMEM((512, 512), BF16),
            pltpu.VMEM((1024, 128), F32),
            pltpu.VMEM((1024, 128), F32),
            pltpu.VMEM((2, 128, 128), BF16),
            pltpu.VMEM((4, 16, 128), BF16),
            pltpu.VMEM((2, 4, 8, 512), BF16),
            pltpu.VMEM((2, 128, 128), BF16),
            pltpu.VMEM((4, 16, 128), BF16),
            pltpu.VMEM((4, 16, 128), F32),
            pltpu.VMEM((2, 128, 128), F32),
            pltpu.VMEM((16, 4, 16, 128), BF16),
            pltpu.VMEM((16, 4, 16, 128), BF16),
            pltpu.VMEM((16, 4, 16, 128), BF16),
            pltpu.VMEM((16, 4, 16, 128), BF16),
            pltpu.VMEM((256, 512), F32),
            dma((6,)), dma((8,)), dma((8,)), dma((16,)), dma((16,)), dma((16,)), dma((16,)),
        ],
        compiler_params=pltpu.CompilerParams(
            collective_id=0, has_side_effects=True, vmem_limit_bytes=60 * 1024 * 1024
        ),
        name="mixing",
    )(latents, spatial_taps, kernel_taps, skip_gain.reshape(1, -1), gate_weight, value_weight)
    result = jnp.dot(hidden, out_weight, preferred_element_type=F32).astype(BF16)
    return result.reshape(latents.shape)


def solution(mesh):
    in_specs = (P("tm", "height", "width", None), P(), P(), P(), P(), P(), P())
    out_specs = P("tm", "height", "width", None)
    return jax.shard_map(body, mesh=mesh, in_specs=in_specs, out_specs=out_specs, check_vma=False)
```

```python
import functools

import jax
import jax.numpy as jnp
from jax import lax
from jax.experimental import pallas as pl
from jax.experimental.pallas import tpu as pltpu
from jax.sharding import PartitionSpec as P

MESH = pl.DeviceIdType.MESH
F32 = jnp.float32
BF16 = jnp.bfloat16
ORDER = (1, 7, 2, 6, 3, 5, 4, 0)
AROUND = ((-1, 0), (1, 0), (0, -1), (0, 1), (-1, -1), (-1, 1), (1, -1), (1, 1))


def owner(group, tile):
    return ((group % 2) * 4 + tile) * 2 + group // 2


def kernel(
    lat, taps, ktaps, skip, wg, wv, hid,
    xl, tv, kt, kf, kb, sk, wgv, wvv, s0, s1, colb, crnb, hrow, hcol, hcrn, hc32, hk32,
    sendb, xin, retb, mixin, gate,
    lsem, hs, hr, fs, fr, rs, rr,
):
    me = lax.axis_index("tm")
    ring, core = me // 2, lax.rem(me, 2)
    hi, wi = lax.axis_index("height"), lax.axis_index("width")
    nh, nw = lax.axis_size("height"), lax.axis_size("width")
    mine = lax.rem(ring, 4)
    lanes = pl.ds(pl.multiple_of(mine * 128, 128), 128)

    loads = [
        pltpu.make_async_copy(lat, xl, lsem.at[0]),
        pltpu.make_async_copy(taps, tv, lsem.at[1]),
        pltpu.make_async_copy(ktaps.at[:, lanes], kt, lsem.at[2]),
        pltpu.make_async_copy(skip.at[:, lanes], sk, lsem.at[3]),
        pltpu.make_async_copy(wg, wgv, lsem.at[4]),
        pltpu.make_async_copy(wv, wvv, lsem.at[5]),
    ]
    loads[0].start()
    loads[1].start()

    def peer(index):
        return (index, hi, wi)

    def beside(step):
        dh, dw = step
        return (me, lax.rem(hi + dh + nh, nh), lax.rem(wi + dw + nw, nw))

    up, down, left, right = hi > 0, hi < nh - 1, wi > 0, wi < nw - 1
    there = (up, down, left, right, up & left, up & right, down & left, down & right)
    count = lambda flag: flag.astype(jnp.int32)
    beside_count = (1 + count(up) + count(down)) * (1 + count(left) + count(right)) - 1

    barrier = pltpu.get_barrier_semaphore()
    for step in range(1, 16):
        pl.semaphore_signal(barrier, inc=1, device_id=peer(lax.rem(me + step, 16)), device_id_type=MESH)
    for step, has in zip(AROUND, there):
        @pl.when(has)
        def _():
            pl.semaphore_signal(barrier, inc=1, device_id=beside(step), device_id_type=MESH)
    for load in loads[2:]:
        load.start()

    loads[0].wait()
    for tile in range(4):
        for frame in range(4):
            at = (tile * 4 + frame) * 64
            s0[at : at + 64] = xl[frame, :, :, tile * 128 : tile * 128 + 128].astype(F32).reshape(64, 128)
    colb[0] = s0[pl.ds(0, 128, stride=8)].astype(BF16)
    colb[1] = s0[pl.ds(7, 128, stride=8)].astype(BF16)
    for n, site in enumerate((0, 7, 56, 63)):
        crnb[n] = s0[pl.ds(site, 16, stride=64)].astype(BF16)

    slots = (hrow.at[0], hrow.at[1], hcol.at[0], hcol.at[1], hcrn.at[0], hcrn.at[1], hcrn.at[2], hcrn.at[3])
    for slot, has in zip(slots, there):
        @pl.when(jnp.logical_not(has))
        def _():
            slot[...] = jnp.zeros(slot.shape, BF16)

    pl.semaphore_wait(barrier, 15 + beside_count)

    pieces = (
        (xl.at[:, 0], hrow.at[1]),
        (xl.at[:, 7], hrow.at[0]),
        (colb.at[0], hcol.at[1]),
        (colb.at[1], hcol.at[0]),
        (crnb.at[0], hcrn.at[3]),
        (crnb.at[1], hcrn.at[2]),
        (crnb.at[2], hcrn.at[1]),
        (crnb.at[3], hcrn.at[0]),
    )
    opposite = (1, 0, 3, 2, 7, 6, 5, 4)
    halo = []
    for n, (src, dst) in enumerate(pieces):
        halo.append(
            pltpu.make_async_remote_copy(
                src_ref=src, dst_ref=dst, send_sem=hs.at[n], recv_sem=hr.at[opposite[n]],
                device_id=beside(AROUND[n]), device_id_type=MESH,
            )
        )
    for copy, has in zip(halo, there):
        pl.when(has)(copy.start)

    sub = lax.broadcasted_iota(jnp.int32, (8, 128), 0)
    first, last = sub == 0, sub == 7
    edge = first | last

    def tap(tile, a, b):
        return tv[a, pl.ds(b, 1), pl.ds(pl.multiple_of(tile * 128, 128), 128)]

    def west(x):
        return jnp.where(first, 0.0, pltpu.roll(x, 1, 0))

    def east(x):
        return jnp.where(last, 0.0, pltpu.roll(x, 7, 0))

    loads[1].wait()

    def inside(i, carry):
        tile, frame = i // 4, lax.rem(i, 4)
        base = pl.multiple_of(i * 64, 64)
        weights = [[tap(tile, a, b) for b in range(3)] for a in range(3)]
        total = [None] * 8
        for r in range(8):
            x = s0[pl.ds(base + r * 8, 8)]
            moved = (west(x), x, east(x))
            for a in range(3):
                o = r + 1 - a
                if 0 <= o < 8:
                    part = weights[a][0] * moved[0] + weights[a][1] * moved[1] + weights[a][2] * moved[2]
                    total[o] = part if total[o] is None else total[o] + part
        for r in (0, 5, 6, 7):
            s1[pl.ds(base + r * 8, 8)] = total[r]
        for r in (1, 2, 3, 4):
            s1[pl.ds(base + r * 8, 8)] = total[r]
        mixed = [
            jnp.where(edge, pltpu.roll(total[5], 6, 0), total[1]),
            jnp.where(edge, pltpu.roll(total[5], 4, 0), total[2]),
            jnp.where(edge, pltpu.roll(total[5], 2, 0), total[3]),
            jnp.where(edge, pltpu.roll(total[6], 6, 0), total[4]),
        ]
        sendb[tile * 2, frame] = jnp.concatenate(mixed[:2], 0).astype(BF16)
        sendb[(4 + tile) * 2, frame] = jnp.concatenate(mixed[2:], 0).astype(BF16)
        return carry

    lax.fori_loop(0, 16, inside, 0)

    def forward(dest):
        return pltpu.make_async_remote_copy(
            src_ref=sendb.at[dest], dst_ref=xin.at[me], send_sem=fs.at[dest], recv_sem=fr.at[me],
            device_id=peer(dest), device_id_type=MESH,
        )

    def keep():
        return pltpu.make_async_copy(sendb.at[me], xin.at[me], fr.at[me])

    def spread(which):
        for step in ORDER:
            dest = lax.rem(ring + step, 8) * 2 + which
            if step:
                forward(dest).start()
            else:
                @pl.when(core == which)
                def _():
                    keep().start()

                @pl.when(core != which)
                def _():
                    forward(dest).start()

    spread(0)

    for n, (src, dst) in enumerate(pieces):
        copy = pltpu.make_async_remote_copy(
            src_ref=src, dst_ref=slots[n], send_sem=hs.at[n], recv_sem=hr.at[n],
            device_id=beside(AROUND[n]), device_id_type=MESH,
        )
        pl.when(there[n])(copy.wait_recv)
    hk32[...] = hcol[...].astype(F32)
    hc32[...] = hcrn[...].astype(F32)

    def border(i, carry):
        tile, frame = i // 4, lax.rem(i, 4)
        base = pl.multiple_of(i * 64, 64)
        chans = pl.ds(pl.multiple_of(tile * 128, 128), 128)
        weights = [[tap(tile, a, b) for b in range(3)] for a in range(3)]
        above = hrow[0, frame, :, chans].astype(F32)
        below = hrow[1, frame, :, chans].astype(F32)
        row0 = s1[pl.ds(base, 8)] + (weights[0][0] * west(above) + weights[0][1] * above + weights[0][2] * east(above))
        row7 = s1[pl.ds(base + 56, 8)] + (weights[2][0] * west(below) + weights[2][1] * below + weights[2][2] * east(below))
        row6 = s1[pl.ds(base + 48, 8)]
        s1[pl.ds(base, 8)] = row0
        s1[pl.ds(base + 56, 8)] = row7
        ends = [
            jnp.where(edge, pltpu.roll(row6, 4, 0), row0),
            jnp.where(edge, pltpu.roll(row6, 2, 0), row7),
        ]
        sides = []
        for n, c in ((0, 0), (1, 7)):
            own = s1[pl.ds(base + c, 8, stride=8)]
            out = hk32[n, pl.ds(pl.multiple_of(i * 8, 8), 8)]
            over = jnp.where(first, hc32[n, pl.ds(i, 1)], pltpu.roll(out, 1, 0))
            under = jnp.where(last, hc32[2 + n, pl.ds(i, 1)], pltpu.roll(out, 7, 0))
            b = 2 * n
            sides.append(own + (weights[0][b] * over + weights[1][b] * out + weights[2][b] * under))
        sendb[tile * 2 + 1, frame] = jnp.concatenate(sides, 0).astype(BF16)
        sendb[(4 + tile) * 2 + 1, frame] = jnp.concatenate(ends, 0).astype(BF16)
        return carry

    lax.fori_loop(0, 16, border, 0)
    spread(1)

    loads[2].wait()
    loads[3].wait()
    kf[...] = kt[...].astype(F32)
    kb[0:8] = jnp.zeros((8, 8, 128), F32)

    def widen(lag, carry):
        kb[8 + lag] = jnp.broadcast_to(kf[pl.ds(lag, 1)], (8, 128))
        return carry

    lax.fori_loop(0, 64, widen, 0)
    kb[8] = kb[8] + jnp.broadcast_to(sk[...], (8, 128))
    loads[4].wait()
    raw = jnp.dot(xl[...].reshape(256, 512), wgv[...], preferred_element_type=F32)
    gate[...] = raw / (1.0 + jnp.exp(-raw))
    loads[5].wait()

    keep().wait()
    for step in range(1, 16):
        src = lax.rem(me + step, 16)
        pltpu.make_async_remote_copy(
            src_ref=sendb.at[src], dst_ref=xin.at[src], send_sem=fs.at[src], recv_sem=fr.at[src],
            device_id=peer(src), device_id_type=MESH,
        ).wait_recv()

    def back(dest):
        return pltpu.make_async_remote_copy(
            src_ref=retb.at[dest], dst_ref=mixin.at[me], send_sem=rs.at[dest], recv_sem=rr.at[me],
            device_id=peer(dest), device_id_type=MESH,
        )

    def own():
        return pltpu.make_async_copy(retb.at[me], mixin.at[me], rr.at[me])

    for step in ORDER:
        chip = lax.rem(ring + step, 8)

        def lagged(source, acc):
            shift = 8 + 8 * (chip - source)
            for s in range(8):
                x = xin[source * 2 + s // 4, s % 4].astype(F32).reshape(1, 2, 8, 128)
                acc = acc + kb[pl.ds(shift - s, 8)].reshape(8, 1, 8, 128) * x
            return acc

        acc = lax.fori_loop(0, chip + 1, lagged, jnp.zeros((8, 2, 8, 128), F32))
        retb[pl.ds(chip * 2, 2)] = acc.reshape(2, 4, 16, 128).astype(BF16)
        if step:
            back(chip * 2).start()
            back(chip * 2 + 1).start()
        else:
            own().start()
            back(chip * 2 + 1 - core).start()

    def arrived(which):
        for step in ORDER:
            src = lax.rem(ring + step, 8) * 2 + which

            def wait():
                pltpu.make_async_remote_copy(
                    src_ref=retb.at[src], dst_ref=mixin.at[src], send_sem=rs.at[src], recv_sem=rr.at[src],
                    device_id=peer(src), device_id_type=MESH,
                ).wait_recv()

            if step:
                wait()
            else:
                pl.when(core == which)(lambda: own().wait())
                pl.when(core != which)(wait)

    def values(which):
        rows = []
        for group in (2 * which, 2 * which + 1):
            rows.append(jnp.concatenate([mixin[owner(group, t)].reshape(64, 128) for t in range(4)], 1))
        return jnp.dot(jnp.concatenate(rows, 0), wvv[...], preferred_element_type=F32)

    def part(block, group, tile, frame, half):
        at = group * 64 + frame * 16 + half * 8
        return block[at : at + 8, tile * 128 : tile * 128 + 128]

    arrived(0)
    v = values(0)
    for tile in range(4):
        for frame in range(4):
            base = (tile * 4 + frame) * 64
            one, two = part(v, 0, tile, frame, 0), part(v, 0, tile, frame, 1)
            three, four = part(v, 1, tile, frame, 0), part(v, 1, tile, frame, 1)
            s1[base + 8 : base + 16] = one
            s1[base + 16 : base + 24] = two
            s1[base + 24 : base + 32] = three
            s1[base + 32 : base + 40] = four
            s1[base + 40 : base + 48] = jnp.where(
                sub < 3, pltpu.roll(one, 2, 0), jnp.where(sub < 5, pltpu.roll(two, 4, 0), pltpu.roll(three, 6, 0))
            )
            s1[base + 48 : base + 56] = pltpu.roll(four, 2, 0)
    arrived(1)
    v = values(1)
    for tile in range(4):
        for frame in range(4):
            base = (tile * 4 + frame) * 64
            top, bottom = part(v, 1, tile, frame, 0), part(v, 1, tile, frame, 1)
            s1[base : base + 8] = top
            s1[base + 56 : base + 64] = bottom
            s1[base + 48 : base + 56] = jnp.where(
                sub < 3, s1[base + 48 : base + 56], jnp.where(sub < 5, pltpu.roll(top, 4, 0), pltpu.roll(bottom, 6, 0))
            )
            s1[pl.ds(base, 8, stride=8)] = part(v, 0, tile, frame, 0)
            s1[pl.ds(base + 7, 8, stride=8)] = part(v, 0, tile, frame, 1)
            rows, chans = slice(frame * 64, frame * 64 + 64), slice(tile * 128, tile * 128 + 128)
            hid[rows, chans] = (s1[base : base + 64] * gate[rows, chans]).astype(BF16)

    for copy, has in zip(halo, there):
        pl.when(has)(copy.wait_send)
    for step in range(1, 16):
        dest = lax.rem(me + step, 16)
        forward(dest).wait_send()
        back(dest).wait_send()


def body(latents, spatial_taps, kernel_taps, skip_gain, gate_weight, value_weight, out_weight):
    dma = pltpu.SemaphoreType.DMA
    hidden = pl.pallas_call(
        kernel,
        out_shape=pltpu.VMEM((256, 512), BF16),
        in_specs=[pl.BlockSpec(memory_space=pl.ANY)] * 6,
        out_specs=pl.BlockSpec(memory_space=pltpu.VMEM),
        scratch_shapes=[
            pltpu.VMEM((4, 8, 8, 512), BF16),
            pltpu.VMEM((3, 3, 512), F32),
            pltpu.VMEM((64, 128), BF16),
            pltpu.VMEM((64, 128), F32),
            pltpu.VMEM((72, 8, 128), F32),
            pltpu.VMEM((1, 128), F32),
            pltpu.VMEM((512, 512), BF16),
            pltpu.VMEM((512, 512), BF16),
            pltpu.VMEM((1024, 128), F32),
            pltpu.VMEM((1024, 128), F32),
            pltpu.VMEM((2, 128, 128), BF16),
            pltpu.VMEM((4, 16, 128), BF16),
            pltpu.VMEM((2, 4, 8, 512), BF16),
            pltpu.VMEM((2, 128, 128), BF16),
            pltpu.VMEM((4, 16, 128), BF16),
            pltpu.VMEM((4, 16, 128), F32),
            pltpu.VMEM((2, 128, 128), F32),
            pltpu.VMEM((16, 4, 16, 128), BF16),
            pltpu.VMEM((16, 4, 16, 128), BF16),
            pltpu.VMEM((16, 4, 16, 128), BF16),
            pltpu.VMEM((16, 4, 16, 128), BF16),
            pltpu.VMEM((256, 512), F32),
            dma((6,)), dma((8,)), dma((8,)), dma((16,)), dma((16,)), dma((16,)), dma((16,)),
        ],
        compiler_params=pltpu.CompilerParams(
            collective_id=0, has_side_effects=True, vmem_limit_bytes=60 * 1024 * 1024
        ),
        name="mixing",
    )(latents, spatial_taps, kernel_taps, skip_gain.reshape(1, -1), gate_weight, value_weight)
    result = jnp.dot(hidden, out_weight, preferred_element_type=F32).astype(BF16)
    return result.reshape(latents.shape)


def solution(mesh):
    in_specs = (P("tm", "height", "width", None), P(), P(), P(), P(), P(), P())
    out_specs = P("tm", "height", "width", None)
    return jax.shard_map(body, mesh=mesh, in_specs=in_specs, out_specs=out_specs, check_vma=False)
```

```python
import functools

import jax
import jax.numpy as jnp
from jax import lax
from jax.experimental import pallas as pl
from jax.experimental.pallas import tpu as pltpu
from jax.sharding import PartitionSpec as P

MESH = pl.DeviceIdType.MESH
F32 = jnp.float32
BF16 = jnp.bfloat16
ORDER = (4, 3, 5, 2, 6, 1, 7, 0)
AROUND = ((-1, 0), (1, 0), (0, -1), (0, 1), (-1, -1), (-1, 1), (1, -1), (1, 1))


def owner(group, tile):
    return ((group % 2) * 4 + tile) * 2 + group // 2


def kernel(
    lat, taps, ktaps, skip, wg, wv, hid,
    xl, tv, kt, kf, kb, sk, wgv, wvv, s0, s1, colb, crnb, hrow, hcol, hcrn, hc32, hk32,
    sendb, xin, retb, mixin, gate,
    lsem, hs, hr, fs, fr, rs, rr,
):
    me = lax.axis_index("tm")
    ring, core = me // 2, lax.rem(me, 2)
    hi, wi = lax.axis_index("height"), lax.axis_index("width")
    nh, nw = lax.axis_size("height"), lax.axis_size("width")
    mine = lax.rem(ring, 4)
    lanes = pl.ds(pl.multiple_of(mine * 128, 128), 128)

    loads = [
        pltpu.make_async_copy(lat, xl, lsem.at[0]),
        pltpu.make_async_copy(taps, tv, lsem.at[1]),
        pltpu.make_async_copy(ktaps.at[:, lanes], kt, lsem.at[2]),
        pltpu.make_async_copy(skip.at[:, lanes], sk, lsem.at[3]),
        pltpu.make_async_copy(wg, wgv, lsem.at[4]),
        pltpu.make_async_copy(wv, wvv, lsem.at[5]),
    ]
    loads[0].start()
    loads[1].start()

    def peer(index):
        return (index, hi, wi)

    def beside(step):
        dh, dw = step
        return (me, lax.rem(hi + dh + nh, nh), lax.rem(wi + dw + nw, nw))

    up, down, left, right = hi > 0, hi < nh - 1, wi > 0, wi < nw - 1
    there = (up, down, left, right, up & left, up & right, down & left, down & right)
    count = lambda flag: flag.astype(jnp.int32)
    beside_count = (1 + count(up) + count(down)) * (1 + count(left) + count(right)) - 1

    barrier = pltpu.get_barrier_semaphore()
    for step in (8, 9, 7, 10, 6, 11, 5, 12, 4, 13, 3, 14, 2, 15, 1):
        pl.semaphore_signal(barrier, inc=1, device_id=peer(lax.rem(me + step, 16)), device_id_type=MESH)
    for step, has in zip(AROUND, there):
        @pl.when(has)
        def _():
            pl.semaphore_signal(barrier, inc=1, device_id=beside(step), device_id_type=MESH)
    for load in loads[2:]:
        load.start()

    loads[0].wait()
    for tile in range(4):
        for frame in range(4):
            at = (tile * 4 + frame) * 64
            s0[at : at + 64] = xl[frame, :, :, tile * 128 : tile * 128 + 128].astype(F32).reshape(64, 128)
    colb[0] = s0[pl.ds(0, 128, stride=8)].astype(BF16)
    colb[1] = s0[pl.ds(7, 128, stride=8)].astype(BF16)
    for n, site in enumerate((0, 7, 56, 63)):
        crnb[n] = s0[pl.ds(site, 16, stride=64)].astype(BF16)

    slots = (hrow.at[0], hrow.at[1], hcol.at[0], hcol.at[1], hcrn.at[0], hcrn.at[1], hcrn.at[2], hcrn.at[3])
    for slot, has in zip(slots, there):
        @pl.when(jnp.logical_not(has))
        def _():
            slot[...] = jnp.zeros(slot.shape, BF16)

    sub = lax.broadcasted_iota(jnp.int32, (8, 128), 0)
    first, last = sub == 0, sub == 7
    edge = first | last

    def tap(tile, a, b):
        return tv[a, pl.ds(b, 1), pl.ds(pl.multiple_of(tile * 128, 128), 128)]

    def west(x):
        return jnp.where(first, 0.0, pltpu.roll(x, 1, 0))

    def east(x):
        return jnp.where(last, 0.0, pltpu.roll(x, 7, 0))

    loads[1].wait()

    def inside(i, carry):
        tile, frame = i // 4, lax.rem(i, 4)
        base = pl.multiple_of(i * 64, 64)
        weights = [[tap(tile, a, b) for b in range(3)] for a in range(3)]
        total = [None] * 8
        for r in range(8):
            x = s0[pl.ds(base + r * 8, 8)]
            moved = (west(x), x, east(x))
            for a in range(3):
                o = r + 1 - a
                if 0 <= o < 8:
                    part = weights[a][0] * moved[0] + weights[a][1] * moved[1] + weights[a][2] * moved[2]
                    total[o] = part if total[o] is None else total[o] + part
        for r in (0, 5, 6, 7):
            s1[pl.ds(base + r * 8, 8)] = total[r]
        for r in (1, 2, 3, 4):
            s1[pl.ds(base + r * 8, 8)] = total[r]
        mixed = [
            jnp.where(edge, pltpu.roll(total[5], 6, 0), total[1]),
            jnp.where(edge, pltpu.roll(total[5], 4, 0), total[2]),
            jnp.where(edge, pltpu.roll(total[5], 2, 0), total[3]),
            jnp.where(edge, pltpu.roll(total[6], 6, 0), total[4]),
        ]
        sendb[tile * 2, frame] = jnp.concatenate(mixed[:2], 0).astype(BF16)
        sendb[(4 + tile) * 2, frame] = jnp.concatenate(mixed[2:], 0).astype(BF16)
        return carry

    lax.fori_loop(0, 16, inside, 0)

    pl.semaphore_wait(barrier, 15 + beside_count)

    pieces = (
        (xl.at[:, 0], hrow.at[1]),
        (xl.at[:, 7], hrow.at[0]),
        (colb.at[0], hcol.at[1]),
        (colb.at[1], hcol.at[0]),
        (crnb.at[0], hcrn.at[3]),
        (crnb.at[1], hcrn.at[2]),
        (crnb.at[2], hcrn.at[1]),
        (crnb.at[3], hcrn.at[0]),
    )
    opposite = (1, 0, 3, 2, 7, 6, 5, 4)
    halo = []
    for n, (src, dst) in enumerate(pieces):
        halo.append(
            pltpu.make_async_remote_copy(
                src_ref=src, dst_ref=dst, send_sem=hs.at[n], recv_sem=hr.at[opposite[n]],
                device_id=beside(AROUND[n]), device_id_type=MESH,
            )
        )
    for copy, has in zip(halo, there):
        pl.when(has)(copy.start)

    def forward(dest):
        return pltpu.make_async_remote_copy(
            src_ref=sendb.at[dest], dst_ref=xin.at[me], send_sem=fs.at[dest], recv_sem=fr.at[me],
            device_id=peer(dest), device_id_type=MESH,
        )

    def keep():
        return pltpu.make_async_copy(sendb.at[me], xin.at[me], fr.at[me])

    def spread(which):
        for step in ORDER:
            dest = lax.rem(ring + step, 8) * 2 + which
            if step:
                forward(dest).start()
            else:
                @pl.when(core == which)
                def _():
                    keep().start()

                @pl.when(core != which)
                def _():
                    forward(dest).start()

    spread(0)

    for n, (src, dst) in enumerate(pieces):
        copy = pltpu.make_async_remote_copy(
            src_ref=src, dst_ref=slots[n], send_sem=hs.at[n], recv_sem=hr.at[n],
            device_id=beside(AROUND[n]), device_id_type=MESH,
        )
        pl.when(there[n])(copy.wait_recv)
    hk32[...] = hcol[...].astype(F32)
    hc32[...] = hcrn[...].astype(F32)

    def border(i, carry):
        tile, frame = i // 4, lax.rem(i, 4)
        base = pl.multiple_of(i * 64, 64)
        chans = pl.ds(pl.multiple_of(tile * 128, 128), 128)
        weights = [[tap(tile, a, b) for b in range(3)] for a in range(3)]
        above = hrow[0, frame, :, chans].astype(F32)
        below = hrow[1, frame, :, chans].astype(F32)
        row0 = s1[pl.ds(base, 8)] + (weights[0][0] * west(above) + weights[0][1] * above + weights[0][2] * east(above))
        row7 = s1[pl.ds(base + 56, 8)] + (weights[2][0] * west(below) + weights[2][1] * below + weights[2][2] * east(below))
        row6 = s1[pl.ds(base + 48, 8)]
        s1[pl.ds(base, 8)] = row0
        s1[pl.ds(base + 56, 8)] = row7
        ends = [
            jnp.where(edge, pltpu.roll(row6, 4, 0), row0),
            jnp.where(edge, pltpu.roll(row6, 2, 0), row7),
        ]
        sides = []
        for n, c in ((0, 0), (1, 7)):
            own = s1[pl.ds(base + c, 8, stride=8)]
            out = hk32[n, pl.ds(pl.multiple_of(i * 8, 8), 8)]
            over = jnp.where(first, hc32[n, pl.ds(i, 1)], pltpu.roll(out, 1, 0))
            under = jnp.where(last, hc32[2 + n, pl.ds(i, 1)], pltpu.roll(out, 7, 0))
            b = 2 * n
            sides.append(own + (weights[0][b] * over + weights[1][b] * out + weights[2][b] * under))
        sendb[tile * 2 + 1, frame] = jnp.concatenate(sides, 0).astype(BF16)
        sendb[(4 + tile) * 2 + 1, frame] = jnp.concatenate(ends, 0).astype(BF16)
        return carry

    lax.fori_loop(0, 16, border, 0)
    spread(1)

    loads[2].wait()
    loads[3].wait()
    kf[...] = kt[...].astype(F32)
    kb[0:8] = jnp.zeros((8, 8, 128), F32)

    def widen(lag, carry):
        kb[8 + lag] = jnp.broadcast_to(kf[pl.ds(lag, 1)], (8, 128))
        return carry

    lax.fori_loop(0, 64, widen, 0)
    kb[8] = kb[8] + jnp.broadcast_to(sk[...], (8, 128))
    loads[4].wait()
    raw = jnp.dot(xl[...].reshape(256, 512), wgv[...], preferred_element_type=F32)
    gate[...] = raw / (1.0 + jnp.exp(-raw))
    loads[5].wait()

    keep().wait()
    for step in range(1, 16):
        src = lax.rem(me + step, 16)
        pltpu.make_async_remote_copy(
            src_ref=sendb.at[src], dst_ref=xin.at[src], send_sem=fs.at[src], recv_sem=fr.at[src],
            device_id=peer(src), device_id_type=MESH,
        ).wait_recv()

    def back(dest):
        return pltpu.make_async_remote_copy(
            src_ref=retb.at[dest], dst_ref=mixin.at[me], send_sem=rs.at[dest], recv_sem=rr.at[me],
            device_id=peer(dest), device_id_type=MESH,
        )

    def own():
        return pltpu.make_async_copy(retb.at[me], mixin.at[me], rr.at[me])

    for step in ORDER:
        chip = lax.rem(ring + step, 8)

        def lagged(source, acc):
            shift = 8 + 8 * (chip - source)
            for s in range(8):
                x = xin[source * 2 + s // 4, s % 4].astype(F32).reshape(1, 2, 8, 128)
                acc = acc + kb[pl.ds(shift - s, 8)].reshape(8, 1, 8, 128) * x
            return acc

        acc = lax.fori_loop(0, chip + 1, lagged, jnp.zeros((8, 2, 8, 128), F32))
        retb[pl.ds(chip * 2, 2)] = acc.reshape(2, 4, 16, 128).astype(BF16)
        if step:
            back(chip * 2).start()
            back(chip * 2 + 1).start()
        else:
            own().start()
            back(chip * 2 + 1 - core).start()

    def arrived(which):
        for step in ORDER:
            src = lax.rem(ring + step, 8) * 2 + which

            def wait():
                pltpu.make_async_remote_copy(
                    src_ref=retb.at[src], dst_ref=mixin.at[src], send_sem=rs.at[src], recv_sem=rr.at[src],
                    device_id=peer(src), device_id_type=MESH,
                ).wait_recv()

            if step:
                wait()
            else:
                pl.when(core == which)(lambda: own().wait())
                pl.when(core != which)(wait)

    def values(which):
        rows = []
        for group in (2 * which, 2 * which + 1):
            rows.append(jnp.concatenate([mixin[owner(group, t)].reshape(64, 128) for t in range(4)], 1))
        return jnp.dot(jnp.concatenate(rows, 0), wvv[...], preferred_element_type=F32)

    def part(block, group, tile, frame, half):
        at = group * 64 + frame * 16 + half * 8
        return block[at : at + 8, tile * 128 : tile * 128 + 128]

    arrived(0)
    v = values(0)
    for tile in range(4):
        for frame in range(4):
            base = (tile * 4 + frame) * 64
            one, two = part(v, 0, tile, frame, 0), part(v, 0, tile, frame, 1)
            three, four = part(v, 1, tile, frame, 0), part(v, 1, tile, frame, 1)
            s1[base + 8 : base + 16] = one
            s1[base + 16 : base + 24] = two
            s1[base + 24 : base + 32] = three
            s1[base + 32 : base + 40] = four
            s1[base + 40 : base + 48] = jnp.where(
                sub < 3, pltpu.roll(one, 2, 0), jnp.where(sub < 5, pltpu.roll(two, 4, 0), pltpu.roll(three, 6, 0))
            )
            s1[base + 48 : base + 56] = pltpu.roll(four, 2, 0)
    arrived(1)
    v = values(1)
    for tile in range(4):
        for frame in range(4):
            base = (tile * 4 + frame) * 64
            top, bottom = part(v, 1, tile, frame, 0), part(v, 1, tile, frame, 1)
            s1[base : base + 8] = top
            s1[base + 56 : base + 64] = bottom
            s1[base + 48 : base + 56] = jnp.where(
                sub < 3, s1[base + 48 : base + 56], jnp.where(sub < 5, pltpu.roll(top, 4, 0), pltpu.roll(bottom, 6, 0))
            )
            s1[pl.ds(base, 8, stride=8)] = part(v, 0, tile, frame, 0)
            s1[pl.ds(base + 7, 8, stride=8)] = part(v, 0, tile, frame, 1)
            rows, chans = slice(frame * 64, frame * 64 + 64), slice(tile * 128, tile * 128 + 128)
            hid[rows, chans] = (s1[base : base + 64] * gate[rows, chans]).astype(BF16)

    for copy, has in zip(halo, there):
        pl.when(has)(copy.wait_send)
    for step in range(1, 16):
        dest = lax.rem(me + step, 16)
        forward(dest).wait_send()
        back(dest).wait_send()


def body(latents, spatial_taps, kernel_taps, skip_gain, gate_weight, value_weight, out_weight):
    dma = pltpu.SemaphoreType.DMA
    hidden = pl.pallas_call(
        kernel,
        out_shape=pltpu.VMEM((256, 512), BF16),
        in_specs=[pl.BlockSpec(memory_space=pl.ANY)] * 6,
        out_specs=pl.BlockSpec(memory_space=pltpu.VMEM),
        scratch_shapes=[
            pltpu.VMEM((4, 8, 8, 512), BF16),
            pltpu.VMEM((3, 3, 512), F32),
            pltpu.VMEM((64, 128), BF16),
            pltpu.VMEM((64, 128), F32),
            pltpu.VMEM((72, 8, 128), F32),
            pltpu.VMEM((1, 128), F32),
            pltpu.VMEM((512, 512), BF16),
            pltpu.VMEM((512, 512), BF16),
            pltpu.VMEM((1024, 128), F32),
            pltpu.VMEM((1024, 128), F32),
            pltpu.VMEM((2, 128, 128), BF16),
            pltpu.VMEM((4, 16, 128), BF16),
            pltpu.VMEM((2, 4, 8, 512), BF16),
            pltpu.VMEM((2, 128, 128), BF16),
            pltpu.VMEM((4, 16, 128), BF16),
            pltpu.VMEM((4, 16, 128), F32),
            pltpu.VMEM((2, 128, 128), F32),
            pltpu.VMEM((16, 4, 16, 128), BF16),
            pltpu.VMEM((16, 4, 16, 128), BF16),
            pltpu.VMEM((16, 4, 16, 128), BF16),
            pltpu.VMEM((16, 4, 16, 128), BF16),
            pltpu.VMEM((256, 512), F32),
            dma((6,)), dma((8,)), dma((8,)), dma((16,)), dma((16,)), dma((16,)), dma((16,)),
        ],
        compiler_params=pltpu.CompilerParams(
            collective_id=0, has_side_effects=True, vmem_limit_bytes=60 * 1024 * 1024
        ),
        name="mixing",
    )(latents, spatial_taps, kernel_taps, skip_gain.reshape(1, -1), gate_weight, value_weight)
    result = jnp.dot(hidden, out_weight, preferred_element_type=F32).astype(BF16)
    return result.reshape(latents.shape)


def solution(mesh):
    in_specs = (P("tm", "height", "width", None), P(), P(), P(), P(), P(), P())
    out_specs = P("tm", "height", "width", None)
    return jax.shard_map(body, mesh=mesh, in_specs=in_specs, out_specs=out_specs, check_vma=False)
```

```python
import functools

import jax
import jax.numpy as jnp
from jax import lax
from jax.experimental import pallas as pl
from jax.experimental.pallas import tpu as pltpu
from jax.sharding import PartitionSpec as P

MESH = pl.DeviceIdType.MESH
F32 = jnp.float32
BF16 = jnp.bfloat16
ORDER = (4, 3, 5, 2, 6, 1, 7, 0)
AROUND = ((-1, 0), (1, 0), (0, -1), (0, 1), (-1, -1), (-1, 1), (1, -1), (1, 1))


def owner(group, tile):
    return ((group % 2) * 4 + tile) * 2 + group // 2


def kernel(
    lat, taps, ktaps, skip, wg, wv, hid,
    xl, tv, kt, kf, kb, sk, wgv, wvv, s0, s1, colb, crnb, hrow, hcol, hcrn, hc32, hk32,
    sendb, xin, retb, mixin, gate,
    lsem, hs, hr, fs, fr, rs, rr,
):
    me = lax.axis_index("tm")
    ring, core = me // 2, lax.rem(me, 2)
    hi, wi = lax.axis_index("height"), lax.axis_index("width")
    nh, nw = lax.axis_size("height"), lax.axis_size("width")
    mine = lax.rem(ring, 4)
    lanes = pl.ds(pl.multiple_of(mine * 128, 128), 128)

    loads = [
        pltpu.make_async_copy(lat, xl, lsem.at[0]),
        pltpu.make_async_copy(taps, tv, lsem.at[1]),
        pltpu.make_async_copy(ktaps.at[:, lanes], kt, lsem.at[2]),
        pltpu.make_async_copy(skip.at[:, lanes], sk, lsem.at[3]),
        pltpu.make_async_copy(wg, wgv, lsem.at[4]),
        pltpu.make_async_copy(wv, wvv, lsem.at[5]),
    ]
    loads[0].start()
    loads[1].start()

    def peer(index):
        return (index, hi, wi)

    def beside(step):
        dh, dw = step
        return (me, lax.rem(hi + dh + nh, nh), lax.rem(wi + dw + nw, nw))

    up, down, left, right = hi > 0, hi < nh - 1, wi > 0, wi < nw - 1
    there = (up, down, left, right, up & left, up & right, down & left, down & right)
    count = lambda flag: flag.astype(jnp.int32)
    beside_count = (1 + count(up) + count(down)) * (1 + count(left) + count(right)) - 1

    barrier = pltpu.get_barrier_semaphore()
    for step in (8, 9, 7, 10, 6, 11, 5, 12, 4, 13, 3, 14, 2, 15, 1):
        pl.semaphore_signal(barrier, inc=1, device_id=peer(lax.rem(me + step, 16)), device_id_type=MESH)
    for step, has in zip(AROUND, there):
        @pl.when(has)
        def _():
            pl.semaphore_signal(barrier, inc=1, device_id=beside(step), device_id_type=MESH)
    for load in loads[2:]:
        load.start()

    loads[0].wait()
    for tile in range(4):
        for frame in range(4):
            at = (tile * 4 + frame) * 64
            s0[at : at + 64] = xl[frame, :, :, tile * 128 : tile * 128 + 128].astype(F32).reshape(64, 128)
    colb[0] = s0[pl.ds(0, 128, stride=8)].astype(BF16)
    colb[1] = s0[pl.ds(7, 128, stride=8)].astype(BF16)
    for n, site in enumerate((0, 7, 56, 63)):
        crnb[n] = s0[pl.ds(site, 16, stride=64)].astype(BF16)

    slots = (hrow.at[0], hrow.at[1], hcol.at[0], hcol.at[1], hcrn.at[0], hcrn.at[1], hcrn.at[2], hcrn.at[3])
    for slot, has in zip(slots, there):
        @pl.when(jnp.logical_not(has))
        def _():
            slot[...] = jnp.zeros(slot.shape, BF16)

    sub = lax.broadcasted_iota(jnp.int32, (8, 128), 0)
    first, last = sub == 0, sub == 7
    edge = first | last

    def tap(tile, a, b):
        return tv[a, pl.ds(b, 1), pl.ds(pl.multiple_of(tile * 128, 128), 128)]

    def west(x):
        return jnp.where(first, 0.0, pltpu.roll(x, 1, 0))

    def east(x):
        return jnp.where(last, 0.0, pltpu.roll(x, 7, 0))

    loads[1].wait()

    def inside(i, carry):
        tile, frame = i // 4, lax.rem(i, 4)
        base = pl.multiple_of(i * 64, 64)
        weights = [[tap(tile, a, b) for b in range(3)] for a in range(3)]
        total = [None] * 8
        for r in range(8):
            x = s0[pl.ds(base + r * 8, 8)]
            moved = (west(x), x, east(x))
            for a in range(3):
                o = r + 1 - a
                if 0 <= o < 8:
                    part = weights[a][0] * moved[0] + weights[a][1] * moved[1] + weights[a][2] * moved[2]
                    total[o] = part if total[o] is None else total[o] + part
        for r in (0, 5, 6, 7):
            s1[pl.ds(base + r * 8, 8)] = total[r]
        for r in (1, 2, 3, 4):
            s1[pl.ds(base + r * 8, 8)] = total[r]
        mixed = [
            jnp.where(edge, pltpu.roll(total[5], 6, 0), total[1]),
            jnp.where(edge, pltpu.roll(total[5], 4, 0), total[2]),
            jnp.where(edge, pltpu.roll(total[5], 2, 0), total[3]),
            jnp.where(edge, pltpu.roll(total[6], 6, 0), total[4]),
        ]
        sendb[tile * 2, frame] = jnp.concatenate(mixed[:2], 0).astype(BF16)
        sendb[(4 + tile) * 2, frame] = jnp.concatenate(mixed[2:], 0).astype(BF16)
        return carry

    lax.fori_loop(0, 16, inside, 0)

    pl.semaphore_wait(barrier, 15 + beside_count)

    pieces = (
        (xl.at[:, 0], hrow.at[1]),
        (xl.at[:, 7], hrow.at[0]),
        (colb.at[0], hcol.at[1]),
        (colb.at[1], hcol.at[0]),
        (crnb.at[0], hcrn.at[3]),
        (crnb.at[1], hcrn.at[2]),
        (crnb.at[2], hcrn.at[1]),
        (crnb.at[3], hcrn.at[0]),
    )
    opposite = (1, 0, 3, 2, 7, 6, 5, 4)
    halo = []
    for n, (src, dst) in enumerate(pieces):
        halo.append(
            pltpu.make_async_remote_copy(
                src_ref=src, dst_ref=dst, send_sem=hs.at[n], recv_sem=hr.at[opposite[n]],
                device_id=beside(AROUND[n]), device_id_type=MESH,
            )
        )
    for copy, has in zip(halo, there):
        pl.when(has)(copy.start)

    def forward(dest):
        return pltpu.make_async_remote_copy(
            src_ref=sendb.at[dest], dst_ref=xin.at[me], send_sem=fs.at[dest], recv_sem=fr.at[me],
            device_id=peer(dest), device_id_type=MESH,
        )

    def keep():
        return pltpu.make_async_copy(sendb.at[me], xin.at[me], fr.at[me])

    def spread(which, turn=None):
        for near, far in zip((4, 2, 6, 0), (3, 5, 1, 7)):
            odd = lax.rem(ring + turn, 2)
            dest = lax.rem(ring + near + odd * (far - near), 8) * 2 + which

            @pl.when(dest == me)
            def _():
                keep().start()

            @pl.when(dest != me)
            def _():
                forward(dest).start()

    spread(0, 0)
    spread(0, 1)

    for n, (src, dst) in enumerate(pieces):
        copy = pltpu.make_async_remote_copy(
            src_ref=src, dst_ref=slots[n], send_sem=hs.at[n], recv_sem=hr.at[n],
            device_id=beside(AROUND[n]), device_id_type=MESH,
        )
        pl.when(there[n])(copy.wait_recv)
    hk32[...] = hcol[...].astype(F32)
    hc32[...] = hcrn[...].astype(F32)

    def border(i, carry):
        tile, frame = i // 4, lax.rem(i, 4)
        base = pl.multiple_of(i * 64, 64)
        chans = pl.ds(pl.multiple_of(tile * 128, 128), 128)
        weights = [[tap(tile, a, b) for b in range(3)] for a in range(3)]
        above = hrow[0, frame, :, chans].astype(F32)
        below = hrow[1, frame, :, chans].astype(F32)
        row0 = s1[pl.ds(base, 8)] + (weights[0][0] * west(above) + weights[0][1] * above + weights[0][2] * east(above))
        row7 = s1[pl.ds(base + 56, 8)] + (weights[2][0] * west(below) + weights[2][1] * below + weights[2][2] * east(below))
        row6 = s1[pl.ds(base + 48, 8)]
        s1[pl.ds(base, 8)] = row0
        s1[pl.ds(base + 56, 8)] = row7
        ends = [
            jnp.where(edge, pltpu.roll(row6, 4, 0), row0),
            jnp.where(edge, pltpu.roll(row6, 2, 0), row7),
        ]
        sides = []
        for n, c in ((0, 0), (1, 7)):
            own = s1[pl.ds(base + c, 8, stride=8)]
            out = hk32[n, pl.ds(pl.multiple_of(i * 8, 8), 8)]
            over = jnp.where(first, hc32[n, pl.ds(i, 1)], pltpu.roll(out, 1, 0))
            under = jnp.where(last, hc32[2 + n, pl.ds(i, 1)], pltpu.roll(out, 7, 0))
            b = 2 * n
            sides.append(own + (weights[0][b] * over + weights[1][b] * out + weights[2][b] * under))
        sendb[tile * 2 + 1, frame] = jnp.concatenate(sides, 0).astype(BF16)
        sendb[(4 + tile) * 2 + 1, frame] = jnp.concatenate(ends, 0).astype(BF16)
        return carry

    lax.fori_loop(0, 16, border, 0)
    spread(1, 0)
    spread(1, 1)

    loads[2].wait()
    loads[3].wait()
    kf[...] = kt[...].astype(F32)
    kb[0:8] = jnp.zeros((8, 8, 128), F32)

    def widen(lag, carry):
        kb[8 + lag] = jnp.broadcast_to(kf[pl.ds(lag, 1)], (8, 128))
        return carry

    lax.fori_loop(0, 64, widen, 0)
    kb[8] = kb[8] + jnp.broadcast_to(sk[...], (8, 128))
    loads[4].wait()
    raw = jnp.dot(xl[...].reshape(256, 512), wgv[...], preferred_element_type=F32)
    gate[...] = raw / (1.0 + jnp.exp(-raw))
    loads[5].wait()

    keep().wait()
    for step in range(1, 16):
        src = lax.rem(me + step, 16)
        pltpu.make_async_remote_copy(
            src_ref=sendb.at[src], dst_ref=xin.at[src], send_sem=fs.at[src], recv_sem=fr.at[src],
            device_id=peer(src), device_id_type=MESH,
        ).wait_recv()

    def back(dest):
        return pltpu.make_async_remote_copy(
            src_ref=retb.at[dest], dst_ref=mixin.at[me], send_sem=rs.at[dest], recv_sem=rr.at[me],
            device_id=peer(dest), device_id_type=MESH,
        )

    def own():
        return pltpu.make_async_copy(retb.at[me], mixin.at[me], rr.at[me])

    for step in (3, 5, 4, 2, 6, 1, 7, 0):
        chip = lax.rem(ring + step, 8)

        def lagged(source, acc):
            shift = 8 + 8 * (chip - source)
            for s in range(8):
                x = xin[source * 2 + s // 4, s % 4].astype(F32).reshape(1, 2, 8, 128)
                acc = acc + kb[pl.ds(shift - s, 8)].reshape(8, 1, 8, 128) * x
            return acc

        acc = lax.fori_loop(0, chip + 1, lagged, jnp.zeros((8, 2, 8, 128), F32))
        retb[pl.ds(chip * 2, 2)] = acc.reshape(2, 4, 16, 128).astype(BF16)
        if step:
            back(chip * 2).start()
            back(chip * 2 + 1).start()
        else:
            own().start()
            back(chip * 2 + 1 - core).start()

    def arrived(which):
        for step in ORDER:
            src = lax.rem(ring + step, 8) * 2 + which

            def wait():
                pltpu.make_async_remote_copy(
                    src_ref=retb.at[src], dst_ref=mixin.at[src], send_sem=rs.at[src], recv_sem=rr.at[src],
                    device_id=peer(src), device_id_type=MESH,
                ).wait_recv()

            if step:
                wait()
            else:
                pl.when(core == which)(lambda: own().wait())
                pl.when(core != which)(wait)

    def values(which):
        rows = []
        for group in (2 * which, 2 * which + 1):
            rows.append(jnp.concatenate([mixin[owner(group, t)].reshape(64, 128) for t in range(4)], 1))
        return jnp.dot(jnp.concatenate(rows, 0), wvv[...], preferred_element_type=F32)

    def part(block, group, tile, frame, half):
        at = group * 64 + frame * 16 + half * 8
        return block[at : at + 8, tile * 128 : tile * 128 + 128]

    arrived(0)
    v = values(0)
    for tile in range(4):
        for frame in range(4):
            base = (tile * 4 + frame) * 64
            one, two = part(v, 0, tile, frame, 0), part(v, 0, tile, frame, 1)
            three, four = part(v, 1, tile, frame, 0), part(v, 1, tile, frame, 1)
            s1[base + 8 : base + 16] = one
            s1[base + 16 : base + 24] = two
            s1[base + 24 : base + 32] = three
            s1[base + 32 : base + 40] = four
            s1[base + 40 : base + 48] = jnp.where(
                sub < 3, pltpu.roll(one, 2, 0), jnp.where(sub < 5, pltpu.roll(two, 4, 0), pltpu.roll(three, 6, 0))
            )
            s1[base + 48 : base + 56] = pltpu.roll(four, 2, 0)
    arrived(1)
    v = values(1)
    for tile in range(4):
        for frame in range(4):
            base = (tile * 4 + frame) * 64
            top, bottom = part(v, 1, tile, frame, 0), part(v, 1, tile, frame, 1)
            s1[base : base + 8] = top
            s1[base + 56 : base + 64] = bottom
            s1[base + 48 : base + 56] = jnp.where(
                sub < 3, s1[base + 48 : base + 56], jnp.where(sub < 5, pltpu.roll(top, 4, 0), pltpu.roll(bottom, 6, 0))
            )
            s1[pl.ds(base, 8, stride=8)] = part(v, 0, tile, frame, 0)
            s1[pl.ds(base + 7, 8, stride=8)] = part(v, 0, tile, frame, 1)
            rows, chans = slice(frame * 64, frame * 64 + 64), slice(tile * 128, tile * 128 + 128)
            hid[rows, chans] = (s1[base : base + 64] * gate[rows, chans]).astype(BF16)

    for copy, has in zip(halo, there):
        pl.when(has)(copy.wait_send)
    for step in range(1, 16):
        dest = lax.rem(me + step, 16)
        forward(dest).wait_send()
        back(dest).wait_send()


def body(latents, spatial_taps, kernel_taps, skip_gain, gate_weight, value_weight, out_weight):
    dma = pltpu.SemaphoreType.DMA
    hidden = pl.pallas_call(
        kernel,
        out_shape=pltpu.VMEM((256, 512), BF16),
        in_specs=[pl.BlockSpec(memory_space=pl.ANY)] * 6,
        out_specs=pl.BlockSpec(memory_space=pltpu.VMEM),
        scratch_shapes=[
            pltpu.VMEM((4, 8, 8, 512), BF16),
            pltpu.VMEM((3, 3, 512), F32),
            pltpu.VMEM((64, 128), BF16),
            pltpu.VMEM((64, 128), F32),
            pltpu.VMEM((72, 8, 128), F32),
            pltpu.VMEM((1, 128), F32),
            pltpu.VMEM((512, 512), BF16),
            pltpu.VMEM((512, 512), BF16),
            pltpu.VMEM((1024, 128), F32),
            pltpu.VMEM((1024, 128), F32),
            pltpu.VMEM((2, 128, 128), BF16),
            pltpu.VMEM((4, 16, 128), BF16),
            pltpu.VMEM((2, 4, 8, 512), BF16),
            pltpu.VMEM((2, 128, 128), BF16),
            pltpu.VMEM((4, 16, 128), BF16),
            pltpu.VMEM((4, 16, 128), F32),
            pltpu.VMEM((2, 128, 128), F32),
            pltpu.VMEM((16, 4, 16, 128), BF16),
            pltpu.VMEM((16, 4, 16, 128), BF16),
            pltpu.VMEM((16, 4, 16, 128), BF16),
            pltpu.VMEM((16, 4, 16, 128), BF16),
            pltpu.VMEM((256, 512), F32),
            dma((6,)), dma((8,)), dma((8,)), dma((16,)), dma((16,)), dma((16,)), dma((16,)),
        ],
        compiler_params=pltpu.CompilerParams(
            collective_id=0, has_side_effects=True, vmem_limit_bytes=60 * 1024 * 1024
        ),
        name="mixing",
    )(latents, spatial_taps, kernel_taps, skip_gain.reshape(1, -1), gate_weight, value_weight)
    result = jnp.dot(hidden, out_weight, preferred_element_type=F32).astype(BF16)
    return result.reshape(latents.shape)


def solution(mesh):
    in_specs = (P("tm", "height", "width", None), P(), P(), P(), P(), P(), P())
    out_specs = P("tm", "height", "width", None)
    return jax.shard_map(body, mesh=mesh, in_specs=in_specs, out_specs=out_specs, check_vma=False)
```

```python
import functools

import jax
import jax.numpy as jnp
from jax import lax
from jax.experimental import pallas as pl
from jax.experimental.pallas import tpu as pltpu
from jax.sharding import PartitionSpec as P

MESH = pl.DeviceIdType.MESH
F32 = jnp.float32
BF16 = jnp.bfloat16
ORDER = (4, 3, 5, 2, 6, 1, 7, 0)
AROUND = ((-1, 0), (1, 0), (0, -1), (0, 1), (-1, -1), (-1, 1), (1, -1), (1, 1))


def owner(group, tile):
    return ((group % 2) * 4 + tile) * 2 + group // 2


def kernel(
    lat, taps, ktaps, skip, wg, wv, hid,
    xl, tv, kt, kf, kb, sk, wgv, wvv, s0, s1, colb, crnb, hrow, hcol, hcrn, hc32, hk32,
    sendb, xin, retb, mixin, gate,
    lsem, hs, hr, fs, fr, rs, rr,
):
    me = lax.axis_index("tm")
    ring, core = me // 2, lax.rem(me, 2)
    hi, wi = lax.axis_index("height"), lax.axis_index("width")
    nh, nw = lax.axis_size("height"), lax.axis_size("width")
    mine = lax.rem(ring, 4)
    lanes = pl.ds(pl.multiple_of(mine * 128, 128), 128)

    loads = [
        pltpu.make_async_copy(lat, xl, lsem.at[0]),
        pltpu.make_async_copy(taps, tv, lsem.at[1]),
        pltpu.make_async_copy(ktaps.at[:, lanes], kt, lsem.at[2]),
        pltpu.make_async_copy(skip.at[:, lanes], sk, lsem.at[3]),
        pltpu.make_async_copy(wg, wgv, lsem.at[4]),
        pltpu.make_async_copy(wv, wvv, lsem.at[5]),
    ]
    loads[0].start()
    loads[1].start()

    def peer(index):
        return (index, hi, wi)

    def beside(step):
        dh, dw = step
        return (me, lax.rem(hi + dh + nh, nh), lax.rem(wi + dw + nw, nw))

    up, down, left, right = hi > 0, hi < nh - 1, wi > 0, wi < nw - 1
    there = (up, down, left, right, up & left, up & right, down & left, down & right)
    count = lambda flag: flag.astype(jnp.int32)
    beside_count = (1 + count(up) + count(down)) * (1 + count(left) + count(right)) - 1

    barrier = pltpu.get_barrier_semaphore()
    for step in (8, 9, 7, 10, 6, 11, 5, 12, 4, 13, 3, 14, 2, 15, 1):
        pl.semaphore_signal(barrier, inc=1, device_id=peer(lax.rem(me + step, 16)), device_id_type=MESH)
    for step, has in zip(AROUND, there):
        @pl.when(has)
        def _():
            pl.semaphore_signal(barrier, inc=1, device_id=beside(step), device_id_type=MESH)
    for load in loads[2:]:
        load.start()

    loads[0].wait()
    for tile in range(4):
        for frame in range(4):
            at = (tile * 4 + frame) * 64
            s0[at : at + 64] = xl[frame, :, :, tile * 128 : tile * 128 + 128].astype(F32).reshape(64, 128)
    colb[0] = s0[pl.ds(0, 128, stride=8)].astype(BF16)
    colb[1] = s0[pl.ds(7, 128, stride=8)].astype(BF16)
    for n, site in enumerate((0, 7, 56, 63)):
        crnb[n] = s0[pl.ds(site, 16, stride=64)].astype(BF16)

    slots = (hrow.at[0], hrow.at[1], hcol.at[0], hcol.at[1], hcrn.at[0], hcrn.at[1], hcrn.at[2], hcrn.at[3])
    for slot, has in zip(slots, there):
        @pl.when(jnp.logical_not(has))
        def _():
            slot[...] = jnp.zeros(slot.shape, BF16)

    sub = lax.broadcasted_iota(jnp.int32, (8, 128), 0)
    first, last = sub == 0, sub == 7
    edge = first | last

    def tap(tile, a, b):
        return tv[a, pl.ds(b, 1), pl.ds(pl.multiple_of(tile * 128, 128), 128)]

    def west(x):
        return jnp.where(first, 0.0, pltpu.roll(x, 1, 0))

    def east(x):
        return jnp.where(last, 0.0, pltpu.roll(x, 7, 0))

    loads[1].wait()

    def inside(i, carry):
        tile, frame = i // 4, lax.rem(i, 4)
        base = pl.multiple_of(i * 64, 64)
        weights = [[tap(tile, a, b) for b in range(3)] for a in range(3)]
        total = [None] * 8
        for r in range(8):
            x = s0[pl.ds(base + r * 8, 8)]
            moved = (west(x), x, east(x))
            for a in range(3):
                o = r + 1 - a
                if 0 <= o < 8:
                    part = weights[a][0] * moved[0] + weights[a][1] * moved[1] + weights[a][2] * moved[2]
                    total[o] = part if total[o] is None else total[o] + part
        for r in (0, 5, 6, 7):
            s1[pl.ds(base + r * 8, 8)] = total[r]
        for r in (1, 2, 3, 4):
            s1[pl.ds(base + r * 8, 8)] = total[r]
        mixed = [
            jnp.where(edge, pltpu.roll(total[5], 6, 0), total[1]),
            jnp.where(edge, pltpu.roll(total[5], 4, 0), total[2]),
            jnp.where(edge, pltpu.roll(total[5], 2, 0), total[3]),
            jnp.where(edge, pltpu.roll(total[6], 6, 0), total[4]),
        ]
        sendb[tile * 2, frame] = jnp.concatenate(mixed[:2], 0).astype(BF16)
        sendb[(4 + tile) * 2, frame] = jnp.concatenate(mixed[2:], 0).astype(BF16)
        return carry

    lax.fori_loop(0, 16, inside, 0)

    pl.semaphore_wait(barrier, 15 + beside_count)

    pieces = (
        (xl.at[:, 0], hrow.at[1]),
        (xl.at[:, 7], hrow.at[0]),
        (colb.at[0], hcol.at[1]),
        (colb.at[1], hcol.at[0]),
        (crnb.at[0], hcrn.at[3]),
        (crnb.at[1], hcrn.at[2]),
        (crnb.at[2], hcrn.at[1]),
        (crnb.at[3], hcrn.at[0]),
    )
    opposite = (1, 0, 3, 2, 7, 6, 5, 4)
    halo = []
    for n, (src, dst) in enumerate(pieces):
        halo.append(
            pltpu.make_async_remote_copy(
                src_ref=src, dst_ref=dst, send_sem=hs.at[n], recv_sem=hr.at[opposite[n]],
                device_id=beside(AROUND[n]), device_id_type=MESH,
            )
        )
    for copy, has in zip(halo, there):
        pl.when(has)(copy.start)

    def forward(dest):
        return pltpu.make_async_remote_copy(
            src_ref=sendb.at[dest], dst_ref=xin.at[me], send_sem=fs.at[dest], recv_sem=fr.at[me],
            device_id=peer(dest), device_id_type=MESH,
        )

    def keep():
        return pltpu.make_async_copy(sendb.at[me], xin.at[me], fr.at[me])

    def spread(which, turn=None):
        for near, far in zip((4, 2, 6, 0), (3, 5, 1, 7)):
            odd = lax.rem(ring + turn, 2)
            dest = lax.rem(ring + near + odd * (far - near), 8) * 2 + which

            @pl.when(dest == me)
            def _():
                keep().start()

            @pl.when(dest != me)
            def _():
                forward(dest).start()

    spread(0, 0)
    spread(0, 1)

    for n, (src, dst) in enumerate(pieces):
        copy = pltpu.make_async_remote_copy(
            src_ref=src, dst_ref=slots[n], send_sem=hs.at[n], recv_sem=hr.at[n],
            device_id=beside(AROUND[n]), device_id_type=MESH,
        )
        pl.when(there[n])(copy.wait_recv)
    hk32[...] = hcol[...].astype(F32)
    hc32[...] = hcrn[...].astype(F32)

    def border(i, carry):
        tile, frame = i // 4, lax.rem(i, 4)
        base = pl.multiple_of(i * 64, 64)
        chans = pl.ds(pl.multiple_of(tile * 128, 128), 128)
        weights = [[tap(tile, a, b) for b in range(3)] for a in range(3)]
        above = hrow[0, frame, :, chans].astype(F32)
        below = hrow[1, frame, :, chans].astype(F32)
        row0 = s1[pl.ds(base, 8)] + (weights[0][0] * west(above) + weights[0][1] * above + weights[0][2] * east(above))
        row7 = s1[pl.ds(base + 56, 8)] + (weights[2][0] * west(below) + weights[2][1] * below + weights[2][2] * east(below))
        row6 = s1[pl.ds(base + 48, 8)]
        s1[pl.ds(base, 8)] = row0
        s1[pl.ds(base + 56, 8)] = row7
        ends = [
            jnp.where(edge, pltpu.roll(row6, 4, 0), row0),
            jnp.where(edge, pltpu.roll(row6, 2, 0), row7),
        ]
        sides = []
        for n, c in ((0, 0), (1, 7)):
            own = s1[pl.ds(base + c, 8, stride=8)]
            out = hk32[n, pl.ds(pl.multiple_of(i * 8, 8), 8)]
            over = jnp.where(first, hc32[n, pl.ds(i, 1)], pltpu.roll(out, 1, 0))
            under = jnp.where(last, hc32[2 + n, pl.ds(i, 1)], pltpu.roll(out, 7, 0))
            b = 2 * n
            sides.append(own + (weights[0][b] * over + weights[1][b] * out + weights[2][b] * under))
        sendb[tile * 2 + 1, frame] = jnp.concatenate(sides, 0).astype(BF16)
        sendb[(4 + tile) * 2 + 1, frame] = jnp.concatenate(ends, 0).astype(BF16)
        return carry

    lax.fori_loop(0, 16, border, 0)
    spread(1, 0)
    spread(1, 1)

    loads[2].wait()
    loads[3].wait()
    kf[...] = kt[...].astype(F32)
    kb[0:8] = jnp.zeros((8, 8, 128), F32)

    def widen(lag, carry):
        kb[8 + lag] = jnp.broadcast_to(kf[pl.ds(lag, 1)], (8, 128))
        return carry

    lax.fori_loop(0, 64, widen, 0)
    kb[8] = kb[8] + jnp.broadcast_to(sk[...], (8, 128))
    loads[4].wait()
    raw = jnp.dot(xl[...].reshape(256, 512), wgv[...], preferred_element_type=F32)
    gate[...] = raw / (1.0 + jnp.exp(-raw))
    loads[5].wait()

    def filtered(src):
        copy = pltpu.make_async_remote_copy(
            src_ref=sendb.at[src], dst_ref=xin.at[src], send_sem=fs.at[src], recv_sem=fr.at[src],
            device_id=peer(src), device_id_type=MESH,
        )
        pl.when(src == me)(lambda: keep().wait())
        pl.when(src != me)(copy.wait_recv)

    def back(dest):
        return pltpu.make_async_remote_copy(
            src_ref=retb.at[dest], dst_ref=mixin.at[me], send_sem=rs.at[dest], recv_sem=rr.at[me],
            device_id=peer(dest), device_id_type=MESH,
        )

    def own():
        return pltpu.make_async_copy(retb.at[me], mixin.at[me], rr.at[me])

    turn = lax.rem(ring + 4, 6)
    for turn_no, chip in enumerate([0, 1] + [2 + lax.rem(turn + step, 6) for step in (3, 2, 4, 1, 5, 0)]):
        if turn_no in (0, 2):
            for src in range(4) if turn_no == 0 else range(4, 16):
                filtered(src)

        def lagged(source, acc):
            shift = 8 + 8 * (chip - source)
            for s in range(8):
                x = xin[source * 2 + s // 4, s % 4].astype(F32).reshape(1, 2, 8, 128)
                acc = acc + kb[pl.ds(shift - s, 8)].reshape(8, 1, 8, 128) * x
            return acc

        acc = lax.fori_loop(0, chip + 1, lagged, jnp.zeros((8, 2, 8, 128), F32))
        retb[pl.ds(chip * 2, 2)] = acc.reshape(2, 4, 16, 128).astype(BF16)
        for dest in (chip * 2, chip * 2 + 1):
            pl.when(dest == me)(lambda: own().start())
            pl.when(dest != me)(back(dest).start)

    def arrived(which):
        for step in ORDER:
            src = lax.rem(ring + step, 8) * 2 + which

            def wait():
                pltpu.make_async_remote_copy(
                    src_ref=retb.at[src], dst_ref=mixin.at[src], send_sem=rs.at[src], recv_sem=rr.at[src],
                    device_id=peer(src), device_id_type=MESH,
                ).wait_recv()

            if step:
                wait()
            else:
                pl.when(core == which)(lambda: own().wait())
                pl.when(core != which)(wait)

    def values(which):
        rows = []
        for group in (2 * which, 2 * which + 1):
            rows.append(jnp.concatenate([mixin[owner(group, t)].reshape(64, 128) for t in range(4)], 1))
        return jnp.dot(jnp.concatenate(rows, 0), wvv[...], preferred_element_type=F32)

    def part(block, group, tile, frame, half):
        at = group * 64 + frame * 16 + half * 8
        return block[at : at + 8, tile * 128 : tile * 128 + 128]

    arrived(0)
    v = values(0)
    for tile in range(4):
        for frame in range(4):
            base = (tile * 4 + frame) * 64
            one, two = part(v, 0, tile, frame, 0), part(v, 0, tile, frame, 1)
            three, four = part(v, 1, tile, frame, 0), part(v, 1, tile, frame, 1)
            s1[base + 8 : base + 16] = one
            s1[base + 16 : base + 24] = two
            s1[base + 24 : base + 32] = three
            s1[base + 32 : base + 40] = four
            s1[base + 40 : base + 48] = jnp.where(
                sub < 3, pltpu.roll(one, 2, 0), jnp.where(sub < 5, pltpu.roll(two, 4, 0), pltpu.roll(three, 6, 0))
            )
            s1[base + 48 : base + 56] = pltpu.roll(four, 2, 0)
    arrived(1)
    v = values(1)
    for tile in range(4):
        for frame in range(4):
            base = (tile * 4 + frame) * 64
            top, bottom = part(v, 1, tile, frame, 0), part(v, 1, tile, frame, 1)
            s1[base : base + 8] = top
            s1[base + 56 : base + 64] = bottom
            s1[base + 48 : base + 56] = jnp.where(
                sub < 3, s1[base + 48 : base + 56], jnp.where(sub < 5, pltpu.roll(top, 4, 0), pltpu.roll(bottom, 6, 0))
            )
            s1[pl.ds(base, 8, stride=8)] = part(v, 0, tile, frame, 0)
            s1[pl.ds(base + 7, 8, stride=8)] = part(v, 0, tile, frame, 1)
            rows, chans = slice(frame * 64, frame * 64 + 64), slice(tile * 128, tile * 128 + 128)
            hid[rows, chans] = (s1[base : base + 64] * gate[rows, chans]).astype(BF16)

    for copy, has in zip(halo, there):
        pl.when(has)(copy.wait_send)
    for step in range(1, 16):
        dest = lax.rem(me + step, 16)
        forward(dest).wait_send()
        back(dest).wait_send()


def body(latents, spatial_taps, kernel_taps, skip_gain, gate_weight, value_weight, out_weight):
    dma = pltpu.SemaphoreType.DMA
    hidden = pl.pallas_call(
        kernel,
        out_shape=pltpu.VMEM((256, 512), BF16),
        in_specs=[pl.BlockSpec(memory_space=pl.ANY)] * 6,
        out_specs=pl.BlockSpec(memory_space=pltpu.VMEM),
        scratch_shapes=[
            pltpu.VMEM((4, 8, 8, 512), BF16),
            pltpu.VMEM((3, 3, 512), F32),
            pltpu.VMEM((64, 128), BF16),
            pltpu.VMEM((64, 128), F32),
            pltpu.VMEM((72, 8, 128), F32),
            pltpu.VMEM((1, 128), F32),
            pltpu.VMEM((512, 512), BF16),
            pltpu.VMEM((512, 512), BF16),
            pltpu.VMEM((1024, 128), F32),
            pltpu.VMEM((1024, 128), F32),
            pltpu.VMEM((2, 128, 128), BF16),
            pltpu.VMEM((4, 16, 128), BF16),
            pltpu.VMEM((2, 4, 8, 512), BF16),
            pltpu.VMEM((2, 128, 128), BF16),
            pltpu.VMEM((4, 16, 128), BF16),
            pltpu.VMEM((4, 16, 128), F32),
            pltpu.VMEM((2, 128, 128), F32),
            pltpu.VMEM((16, 4, 16, 128), BF16),
            pltpu.VMEM((16, 4, 16, 128), BF16),
            pltpu.VMEM((16, 4, 16, 128), BF16),
            pltpu.VMEM((16, 4, 16, 128), BF16),
            pltpu.VMEM((256, 512), F32),
            dma((6,)), dma((8,)), dma((8,)), dma((16,)), dma((16,)), dma((16,)), dma((16,)),
        ],
        compiler_params=pltpu.CompilerParams(
            collective_id=0, has_side_effects=True, vmem_limit_bytes=60 * 1024 * 1024
        ),
        name="mixing",
    )(latents, spatial_taps, kernel_taps, skip_gain.reshape(1, -1), gate_weight, value_weight)
    result = jnp.dot(hidden, out_weight, preferred_element_type=F32).astype(BF16)
    return result.reshape(latents.shape)


def solution(mesh):
    in_specs = (P("tm", "height", "width", None), P(), P(), P(), P(), P(), P())
    out_specs = P("tm", "height", "width", None)
    return jax.shard_map(body, mesh=mesh, in_specs=in_specs, out_specs=out_specs, check_vma=False)
```

```python
import functools

import jax
import jax.numpy as jnp
from jax import lax
from jax.experimental import pallas as pl
from jax.experimental.pallas import tpu as pltpu
from jax.sharding import PartitionSpec as P

MESH = pl.DeviceIdType.MESH
F32 = jnp.float32
BF16 = jnp.bfloat16
ORDER = (4, 3, 5, 2, 6, 1, 7, 0)
AROUND = ((-1, 0), (1, 0), (0, -1), (0, 1), (-1, -1), (-1, 1), (1, -1), (1, 1))


def owner(group, tile):
    return ((group % 2) * 4 + tile) * 2 + group // 2


def kernel(
    lat, taps, ktaps, skip, wg, wv, hid,
    xl, tv, kt, kf, kb, sk, wgv, wvv, s0, s1, colb, crnb, hrow, hcol, hcrn, hc32, hk32,
    sendb, xin, retb, mixin, gate,
    lsem, hs, hr, fs, fr, rs, rr,
):
    me = lax.axis_index("tm")
    ring, core = me // 2, lax.rem(me, 2)
    hi, wi = lax.axis_index("height"), lax.axis_index("width")
    nh, nw = lax.axis_size("height"), lax.axis_size("width")
    mine = lax.rem(ring, 4)
    lanes = pl.ds(pl.multiple_of(mine * 128, 128), 128)

    loads = [
        pltpu.make_async_copy(lat, xl, lsem.at[0]),
        pltpu.make_async_copy(taps, tv, lsem.at[1]),
        pltpu.make_async_copy(ktaps.at[:, lanes], kt, lsem.at[2]),
        pltpu.make_async_copy(skip.at[:, lanes], sk, lsem.at[3]),
        pltpu.make_async_copy(wg, wgv, lsem.at[4]),
        pltpu.make_async_copy(wv, wvv, lsem.at[5]),
    ]
    loads[0].start()
    loads[1].start()

    def peer(index):
        return (index, hi, wi)

    def beside(step):
        dh, dw = step
        return (me, lax.rem(hi + dh + nh, nh), lax.rem(wi + dw + nw, nw))

    up, down, left, right = hi > 0, hi < nh - 1, wi > 0, wi < nw - 1
    there = (up, down, left, right, up & left, up & right, down & left, down & right)
    count = lambda flag: flag.astype(jnp.int32)
    beside_count = (1 + count(up) + count(down)) * (1 + count(left) + count(right)) - 1

    barrier = pltpu.get_barrier_semaphore()
    for step in (8, 9, 7, 10, 6, 11, 5, 12, 4, 13, 3, 14, 2, 15, 1):
        pl.semaphore_signal(barrier, inc=1, device_id=peer(lax.rem(me + step, 16)), device_id_type=MESH)
    for step, has in zip(AROUND, there):
        @pl.when(has)
        def _():
            pl.semaphore_signal(barrier, inc=1, device_id=beside(step), device_id_type=MESH)
    for load in loads[2:]:
        load.start()

    loads[0].wait()
    for tile in range(4):
        for frame in range(4):
            at = (tile * 4 + frame) * 64
            s0[at : at + 64] = xl[frame, :, :, tile * 128 : tile * 128 + 128].astype(F32).reshape(64, 128)
    colb[0] = s0[pl.ds(0, 128, stride=8)].astype(BF16)
    colb[1] = s0[pl.ds(7, 128, stride=8)].astype(BF16)
    for n, site in enumerate((0, 7, 56, 63)):
        crnb[n] = s0[pl.ds(site, 16, stride=64)].astype(BF16)

    slots = (hrow.at[0], hrow.at[1], hcol.at[0], hcol.at[1], hcrn.at[0], hcrn.at[1], hcrn.at[2], hcrn.at[3])
    for slot, has in zip(slots, there):
        @pl.when(jnp.logical_not(has))
        def _():
            slot[...] = jnp.zeros(slot.shape, BF16)

    sub = lax.broadcasted_iota(jnp.int32, (8, 128), 0)
    first, last = sub == 0, sub == 7
    edge = first | last

    def tap(tile, a, b):
        return tv[a, pl.ds(b, 1), pl.ds(pl.multiple_of(tile * 128, 128), 128)]

    def west(x):
        return jnp.where(first, 0.0, pltpu.roll(x, 1, 0))

    def east(x):
        return jnp.where(last, 0.0, pltpu.roll(x, 7, 0))

    loads[1].wait()

    def inside(i, carry):
        tile, frame = i // 4, lax.rem(i, 4)
        base = pl.multiple_of(i * 64, 64)
        weights = [[tap(tile, a, b) for b in range(3)] for a in range(3)]
        total = [None] * 8
        for r in range(8):
            x = s0[pl.ds(base + r * 8, 8)]
            moved = (west(x), x, east(x))
            for a in range(3):
                o = r + 1 - a
                if 0 <= o < 8:
                    part = weights[a][0] * moved[0] + weights[a][1] * moved[1] + weights[a][2] * moved[2]
                    total[o] = part if total[o] is None else total[o] + part
        for r in (0, 5, 6, 7):
            s1[pl.ds(base + r * 8, 8)] = total[r]
        for r in (1, 2, 3, 4):
            s1[pl.ds(base + r * 8, 8)] = total[r]
        mixed = [
            jnp.where(edge, pltpu.roll(total[5], 6, 0), total[1]),
            jnp.where(edge, pltpu.roll(total[5], 4, 0), total[2]),
            jnp.where(edge, pltpu.roll(total[5], 2, 0), total[3]),
            jnp.where(edge, pltpu.roll(total[6], 6, 0), total[4]),
        ]
        sendb[tile * 2, frame] = jnp.concatenate(mixed[:2], 0).astype(BF16)
        sendb[(4 + tile) * 2, frame] = jnp.concatenate(mixed[2:], 0).astype(BF16)
        return carry

    lax.fori_loop(0, 16, inside, 0)

    pl.semaphore_wait(barrier, 15 + beside_count)

    pieces = (
        (xl.at[:, 0], hrow.at[1]),
        (xl.at[:, 7], hrow.at[0]),
        (colb.at[0], hcol.at[1]),
        (colb.at[1], hcol.at[0]),
        (crnb.at[0], hcrn.at[3]),
        (crnb.at[1], hcrn.at[2]),
        (crnb.at[2], hcrn.at[1]),
        (crnb.at[3], hcrn.at[0]),
    )
    opposite = (1, 0, 3, 2, 7, 6, 5, 4)
    halo = []
    for n, (src, dst) in enumerate(pieces):
        halo.append(
            pltpu.make_async_remote_copy(
                src_ref=src, dst_ref=dst, send_sem=hs.at[n], recv_sem=hr.at[opposite[n]],
                device_id=beside(AROUND[n]), device_id_type=MESH,
            )
        )
    for copy, has in zip(halo, there):
        pl.when(has)(copy.start)

    def forward(dest):
        return pltpu.make_async_remote_copy(
            src_ref=sendb.at[dest], dst_ref=xin.at[me], send_sem=fs.at[dest], recv_sem=fr.at[me],
            device_id=peer(dest), device_id_type=MESH,
        )

    def keep():
        return pltpu.make_async_copy(sendb.at[me], xin.at[me], fr.at[me])

    def spread(which):
        chips = []
        for step in range(4):
            chip = step
            apart = lax.rem(ring - chip + 8, 8)
            near = 4 * ((apart < 2) | (apart > 6)).astype(jnp.int32)
            chips += [chip + near, chip + 4 - near]
        for dest in [chip * 2 + which for chip in chips]:

            @pl.when(dest == me)
            def _():
                keep().start()

            @pl.when(dest != me)
            def _():
                forward(dest).start()

    spread(0)

    for n, (src, dst) in enumerate(pieces):
        copy = pltpu.make_async_remote_copy(
            src_ref=src, dst_ref=slots[n], send_sem=hs.at[n], recv_sem=hr.at[n],
            device_id=beside(AROUND[n]), device_id_type=MESH,
        )
        pl.when(there[n])(copy.wait_recv)
    hk32[...] = hcol[...].astype(F32)
    hc32[...] = hcrn[...].astype(F32)

    def border(i, carry):
        tile, frame = i // 4, lax.rem(i, 4)
        base = pl.multiple_of(i * 64, 64)
        chans = pl.ds(pl.multiple_of(tile * 128, 128), 128)
        weights = [[tap(tile, a, b) for b in range(3)] for a in range(3)]
        above = hrow[0, frame, :, chans].astype(F32)
        below = hrow[1, frame, :, chans].astype(F32)
        row0 = s1[pl.ds(base, 8)] + (weights[0][0] * west(above) + weights[0][1] * above + weights[0][2] * east(above))
        row7 = s1[pl.ds(base + 56, 8)] + (weights[2][0] * west(below) + weights[2][1] * below + weights[2][2] * east(below))
        row6 = s1[pl.ds(base + 48, 8)]
        s1[pl.ds(base, 8)] = row0
        s1[pl.ds(base + 56, 8)] = row7
        ends = [
            jnp.where(edge, pltpu.roll(row6, 4, 0), row0),
            jnp.where(edge, pltpu.roll(row6, 2, 0), row7),
        ]
        sides = []
        for n, c in ((0, 0), (1, 7)):
            own = s1[pl.ds(base + c, 8, stride=8)]
            out = hk32[n, pl.ds(pl.multiple_of(i * 8, 8), 8)]
            over = jnp.where(first, hc32[n, pl.ds(i, 1)], pltpu.roll(out, 1, 0))
            under = jnp.where(last, hc32[2 + n, pl.ds(i, 1)], pltpu.roll(out, 7, 0))
            b = 2 * n
            sides.append(own + (weights[0][b] * over + weights[1][b] * out + weights[2][b] * under))
        sendb[tile * 2 + 1, frame] = jnp.concatenate(sides, 0).astype(BF16)
        sendb[(4 + tile) * 2 + 1, frame] = jnp.concatenate(ends, 0).astype(BF16)
        return carry

    lax.fori_loop(0, 16, border, 0)
    spread(1)

    loads[2].wait()
    loads[3].wait()
    kf[...] = kt[...].astype(F32)
    kb[0:8] = jnp.zeros((8, 8, 128), F32)

    def widen(lag, carry):
        kb[8 + lag] = jnp.broadcast_to(kf[pl.ds(lag, 1)], (8, 128))
        return carry

    lax.fori_loop(0, 64, widen, 0)
    kb[8] = kb[8] + jnp.broadcast_to(sk[...], (8, 128))
    loads[4].wait()
    raw = jnp.dot(xl[...].reshape(256, 512), wgv[...], preferred_element_type=F32)
    gate[...] = raw / (1.0 + jnp.exp(-raw))
    loads[5].wait()

    def filtered(src):
        copy = pltpu.make_async_remote_copy(
            src_ref=sendb.at[src], dst_ref=xin.at[src], send_sem=fs.at[src], recv_sem=fr.at[src],
            device_id=peer(src), device_id_type=MESH,
        )
        pl.when(src == me)(lambda: keep().wait())
        pl.when(src != me)(copy.wait_recv)

    def back(dest):
        return pltpu.make_async_remote_copy(
            src_ref=retb.at[dest], dst_ref=mixin.at[me], send_sem=rs.at[dest], recv_sem=rr.at[me],
            device_id=peer(dest), device_id_type=MESH,
        )

    def own():
        return pltpu.make_async_copy(retb.at[me], mixin.at[me], rr.at[me])

    turn = lax.rem(ring + 4, 6)
    for turn_no, chip in enumerate([0, 1] + [2 + lax.rem(turn + step, 6) for step in (3, 2, 4, 1, 5, 0)]):
        if turn_no in (0, 2):
            for src in range(4) if turn_no == 0 else range(4, 16):
                filtered(src)

        def lagged(source, acc):
            shift = 8 + 8 * (chip - source)
            for s in range(8):
                x = xin[source * 2 + s // 4, s % 4].astype(F32).reshape(1, 2, 8, 128)
                acc = acc + kb[pl.ds(shift - s, 8)].reshape(8, 1, 8, 128) * x
            return acc

        acc = lax.fori_loop(0, chip + 1, lagged, jnp.zeros((8, 2, 8, 128), F32))
        retb[pl.ds(chip * 2, 2)] = acc.reshape(2, 4, 16, 128).astype(BF16)
        for dest in (chip * 2, chip * 2 + 1):
            pl.when(dest == me)(lambda: own().start())
            pl.when(dest != me)(back(dest).start)

    def arrived(which):
        for step in ORDER:
            src = lax.rem(ring + step, 8) * 2 + which

            def wait():
                pltpu.make_async_remote_copy(
                    src_ref=retb.at[src], dst_ref=mixin.at[src], send_sem=rs.at[src], recv_sem=rr.at[src],
                    device_id=peer(src), device_id_type=MESH,
                ).wait_recv()

            if step:
                wait()
            else:
                pl.when(core == which)(lambda: own().wait())
                pl.when(core != which)(wait)

    def values(which):
        rows = []
        for group in (2 * which, 2 * which + 1):
            rows.append(jnp.concatenate([mixin[owner(group, t)].reshape(64, 128) for t in range(4)], 1))
        return jnp.dot(jnp.concatenate(rows, 0), wvv[...], preferred_element_type=F32)

    def part(block, group, tile, frame, half):
        at = group * 64 + frame * 16 + half * 8
        return block[at : at + 8, tile * 128 : tile * 128 + 128]

    arrived(0)
    v = values(0)
    for tile in range(4):
        for frame in range(4):
            base = (tile * 4 + frame) * 64
            one, two = part(v, 0, tile, frame, 0), part(v, 0, tile, frame, 1)
            three, four = part(v, 1, tile, frame, 0), part(v, 1, tile, frame, 1)
            s1[base + 8 : base + 16] = one
            s1[base + 16 : base + 24] = two
            s1[base + 24 : base + 32] = three
            s1[base + 32 : base + 40] = four
            s1[base + 40 : base + 48] = jnp.where(
                sub < 3, pltpu.roll(one, 2, 0), jnp.where(sub < 5, pltpu.roll(two, 4, 0), pltpu.roll(three, 6, 0))
            )
            s1[base + 48 : base + 56] = pltpu.roll(four, 2, 0)
    arrived(1)
    v = values(1)
    for tile in range(4):
        for frame in range(4):
            base = (tile * 4 + frame) * 64
            top, bottom = part(v, 1, tile, frame, 0), part(v, 1, tile, frame, 1)
            s1[base : base + 8] = top
            s1[base + 56 : base + 64] = bottom
            s1[base + 48 : base + 56] = jnp.where(
                sub < 3, s1[base + 48 : base + 56], jnp.where(sub < 5, pltpu.roll(top, 4, 0), pltpu.roll(bottom, 6, 0))
            )
            s1[pl.ds(base, 8, stride=8)] = part(v, 0, tile, frame, 0)
            s1[pl.ds(base + 7, 8, stride=8)] = part(v, 0, tile, frame, 1)
            rows, chans = slice(frame * 64, frame * 64 + 64), slice(tile * 128, tile * 128 + 128)
            hid[rows, chans] = (s1[base : base + 64] * gate[rows, chans]).astype(BF16)

    for copy, has in zip(halo, there):
        pl.when(has)(copy.wait_send)
    for step in range(1, 16):
        dest = lax.rem(me + step, 16)
        forward(dest).wait_send()
        back(dest).wait_send()


def body(latents, spatial_taps, kernel_taps, skip_gain, gate_weight, value_weight, out_weight):
    dma = pltpu.SemaphoreType.DMA
    hidden = pl.pallas_call(
        kernel,
        out_shape=pltpu.VMEM((256, 512), BF16),
        in_specs=[pl.BlockSpec(memory_space=pl.ANY)] * 6,
        out_specs=pl.BlockSpec(memory_space=pltpu.VMEM),
        scratch_shapes=[
            pltpu.VMEM((4, 8, 8, 512), BF16),
            pltpu.VMEM((3, 3, 512), F32),
            pltpu.VMEM((64, 128), BF16),
            pltpu.VMEM((64, 128), F32),
            pltpu.VMEM((72, 8, 128), F32),
            pltpu.VMEM((1, 128), F32),
            pltpu.VMEM((512, 512), BF16),
            pltpu.VMEM((512, 512), BF16),
            pltpu.VMEM((1024, 128), F32),
            pltpu.VMEM((1024, 128), F32),
            pltpu.VMEM((2, 128, 128), BF16),
            pltpu.VMEM((4, 16, 128), BF16),
            pltpu.VMEM((2, 4, 8, 512), BF16),
            pltpu.VMEM((2, 128, 128), BF16),
            pltpu.VMEM((4, 16, 128), BF16),
            pltpu.VMEM((4, 16, 128), F32),
            pltpu.VMEM((2, 128, 128), F32),
            pltpu.VMEM((16, 4, 16, 128), BF16),
            pltpu.VMEM((16, 4, 16, 128), BF16),
            pltpu.VMEM((16, 4, 16, 128), BF16),
            pltpu.VMEM((16, 4, 16, 128), BF16),
            pltpu.VMEM((256, 512), F32),
            dma((6,)), dma((8,)), dma((8,)), dma((16,)), dma((16,)), dma((16,)), dma((16,)),
        ],
        compiler_params=pltpu.CompilerParams(
            collective_id=0, has_side_effects=True, vmem_limit_bytes=60 * 1024 * 1024
        ),
        name="mixing",
    )(latents, spatial_taps, kernel_taps, skip_gain.reshape(1, -1), gate_weight, value_weight)
    result = jnp.dot(hidden, out_weight, preferred_element_type=F32).astype(BF16)
    return result.reshape(latents.shape)


def solution(mesh):
    in_specs = (P("tm", "height", "width", None), P(), P(), P(), P(), P(), P())
    out_specs = P("tm", "height", "width", None)
    return jax.shard_map(body, mesh=mesh, in_specs=in_specs, out_specs=out_specs, check_vma=False)
```

```python
import functools

import jax
import jax.numpy as jnp
from jax import lax
from jax.experimental import pallas as pl
from jax.experimental.pallas import tpu as pltpu
from jax.sharding import PartitionSpec as P

MESH = pl.DeviceIdType.MESH
F32 = jnp.float32
BF16 = jnp.bfloat16
ORDER = (4, 3, 5, 2, 6, 1, 7, 0)
AROUND = ((-1, 0), (1, 0), (0, -1), (0, 1), (-1, -1), (-1, 1), (1, -1), (1, 1))


def owner(group, tile):
    return ((group % 2) * 4 + tile) * 2 + group // 2


def kernel(
    lat, taps, ktaps, skip, wg, wv, hid,
    xl, tv, kt, kf, kb, sk, wgv, wvv, s0, s1, colb, crnb, hrow, hcol, hcrn, hc32, hk32,
    sendb, xin, retb, mixin, gate,
    lsem, hs, hr, fs, fr, rs, rr,
):
    me = lax.axis_index("tm")
    ring, core = me // 2, lax.rem(me, 2)
    hi, wi = lax.axis_index("height"), lax.axis_index("width")
    nh, nw = lax.axis_size("height"), lax.axis_size("width")
    mine = lax.rem(ring, 4)
    lanes = pl.ds(pl.multiple_of(mine * 128, 128), 128)

    loads = [
        pltpu.make_async_copy(lat, xl, lsem.at[0]),
        pltpu.make_async_copy(taps, tv, lsem.at[1]),
        pltpu.make_async_copy(ktaps.at[:, lanes], kt, lsem.at[2]),
        pltpu.make_async_copy(skip.at[:, lanes], sk, lsem.at[3]),
        pltpu.make_async_copy(wg, wgv, lsem.at[4]),
        pltpu.make_async_copy(wv, wvv, lsem.at[5]),
    ]
    loads[0].start()
    loads[1].start()

    def peer(index):
        return (index, hi, wi)

    def beside(step):
        dh, dw = step
        return (me, lax.rem(hi + dh + nh, nh), lax.rem(wi + dw + nw, nw))

    up, down, left, right = hi > 0, hi < nh - 1, wi > 0, wi < nw - 1
    there = (up, down, left, right, up & left, up & right, down & left, down & right)
    count = lambda flag: flag.astype(jnp.int32)
    beside_count = (1 + count(up) + count(down)) * (1 + count(left) + count(right)) - 1

    barrier = pltpu.get_barrier_semaphore()
    for step in (8, 9, 7, 10, 6, 11, 5, 12, 4, 13, 3, 14, 2, 15, 1):
        pl.semaphore_signal(barrier, inc=1, device_id=peer(lax.rem(me + step, 16)), device_id_type=MESH)
    for step, has in zip(AROUND, there):
        @pl.when(has)
        def _():
            pl.semaphore_signal(barrier, inc=1, device_id=beside(step), device_id_type=MESH)
    for load in loads[2:]:
        load.start()

    loads[0].wait()
    for tile in range(4):
        for frame in range(4):
            at = (tile * 4 + frame) * 64
            s0[at : at + 64] = xl[frame, :, :, tile * 128 : tile * 128 + 128].astype(F32).reshape(64, 128)
    colb[0] = s0[pl.ds(0, 128, stride=8)].astype(BF16)
    colb[1] = s0[pl.ds(7, 128, stride=8)].astype(BF16)
    for n, site in enumerate((0, 7, 56, 63)):
        crnb[n] = s0[pl.ds(site, 16, stride=64)].astype(BF16)

    slots = (hrow.at[0], hrow.at[1], hcol.at[0], hcol.at[1], hcrn.at[0], hcrn.at[1], hcrn.at[2], hcrn.at[3])
    for slot, has in zip(slots, there):
        @pl.when(jnp.logical_not(has))
        def _():
            slot[...] = jnp.zeros(slot.shape, BF16)

    sub = lax.broadcasted_iota(jnp.int32, (8, 128), 0)
    first, last = sub == 0, sub == 7
    edge = first | last

    def tap(tile, a, b):
        return tv[a, pl.ds(b, 1), pl.ds(pl.multiple_of(tile * 128, 128), 128)]

    def west(x):
        return jnp.where(first, 0.0, pltpu.roll(x, 1, 0))

    def east(x):
        return jnp.where(last, 0.0, pltpu.roll(x, 7, 0))

    loads[1].wait()

    def inside(i, carry):
        tile, frame = i // 4, lax.rem(i, 4)
        base = pl.multiple_of(i * 64, 64)
        weights = [[tap(tile, a, b) for b in range(3)] for a in range(3)]
        total = [None] * 8
        for r in range(8):
            x = s0[pl.ds(base + r * 8, 8)]
            moved = (west(x), x, east(x))
            for a in range(3):
                o = r + 1 - a
                if 0 <= o < 8:
                    part = weights[a][0] * moved[0] + weights[a][1] * moved[1] + weights[a][2] * moved[2]
                    total[o] = part if total[o] is None else total[o] + part
        for r in (0, 5, 6, 7):
            s1[pl.ds(base + r * 8, 8)] = total[r]
        for r in (1, 2, 3, 4):
            s1[pl.ds(base + r * 8, 8)] = total[r]
        mixed = [
            jnp.where(edge, pltpu.roll(total[5], 6, 0), total[1]),
            jnp.where(edge, pltpu.roll(total[5], 4, 0), total[2]),
            jnp.where(edge, pltpu.roll(total[5], 2, 0), total[3]),
            jnp.where(edge, pltpu.roll(total[6], 6, 0), total[4]),
        ]
        sendb[tile * 2, frame] = jnp.concatenate(mixed[:2], 0).astype(BF16)
        sendb[(4 + tile) * 2, frame] = jnp.concatenate(mixed[2:], 0).astype(BF16)
        return carry

    lax.fori_loop(0, 16, inside, 0)

    pl.semaphore_wait(barrier, 15 + beside_count)

    pieces = (
        (xl.at[:, 0], hrow.at[1]),
        (xl.at[:, 7], hrow.at[0]),
        (colb.at[0], hcol.at[1]),
        (colb.at[1], hcol.at[0]),
        (crnb.at[0], hcrn.at[3]),
        (crnb.at[1], hcrn.at[2]),
        (crnb.at[2], hcrn.at[1]),
        (crnb.at[3], hcrn.at[0]),
    )
    opposite = (1, 0, 3, 2, 7, 6, 5, 4)
    halo = []
    for n, (src, dst) in enumerate(pieces):
        halo.append(
            pltpu.make_async_remote_copy(
                src_ref=src, dst_ref=dst, send_sem=hs.at[n], recv_sem=hr.at[opposite[n]],
                device_id=beside(AROUND[n]), device_id_type=MESH,
            )
        )
    for copy, has in zip(halo, there):
        pl.when(has)(copy.start)

    def forward(dest):
        return pltpu.make_async_remote_copy(
            src_ref=sendb.at[dest], dst_ref=xin.at[me], send_sem=fs.at[dest], recv_sem=fr.at[me],
            device_id=peer(dest), device_id_type=MESH,
        )

    def keep():
        return pltpu.make_async_copy(sendb.at[me], xin.at[me], fr.at[me])

    def spread(which, turn=None):
        for near, far in zip((4, 2, 6, 0), (3, 5, 1, 7)):
            odd = lax.rem(ring + turn, 2)
            dest = lax.rem(ring + near + odd * (far - near), 8) * 2 + which

            @pl.when(dest == me)
            def _():
                keep().start()

            @pl.when(dest != me)
            def _():
                forward(dest).start()

    spread(0, 0)
    spread(0, 1)

    for n, (src, dst) in enumerate(pieces):
        copy = pltpu.make_async_remote_copy(
            src_ref=src, dst_ref=slots[n], send_sem=hs.at[n], recv_sem=hr.at[n],
            device_id=beside(AROUND[n]), device_id_type=MESH,
        )
        pl.when(there[n])(copy.wait_recv)
    hk32[...] = hcol[...].astype(F32)
    hc32[...] = hcrn[...].astype(F32)

    def border(i, carry):
        tile, frame = i // 4, lax.rem(i, 4)
        base = pl.multiple_of(i * 64, 64)
        chans = pl.ds(pl.multiple_of(tile * 128, 128), 128)
        weights = [[tap(tile, a, b) for b in range(3)] for a in range(3)]
        above = hrow[0, frame, :, chans].astype(F32)
        below = hrow[1, frame, :, chans].astype(F32)
        row0 = s1[pl.ds(base, 8)] + (weights[0][0] * west(above) + weights[0][1] * above + weights[0][2] * east(above))
        row7 = s1[pl.ds(base + 56, 8)] + (weights[2][0] * west(below) + weights[2][1] * below + weights[2][2] * east(below))
        row6 = s1[pl.ds(base + 48, 8)]
        s1[pl.ds(base, 8)] = row0
        s1[pl.ds(base + 56, 8)] = row7
        ends = [
            jnp.where(edge, pltpu.roll(row6, 4, 0), row0),
            jnp.where(edge, pltpu.roll(row6, 2, 0), row7),
        ]
        sides = []
        for n, c in ((0, 0), (1, 7)):
            own = s1[pl.ds(base + c, 8, stride=8)]
            out = hk32[n, pl.ds(pl.multiple_of(i * 8, 8), 8)]
            over = jnp.where(first, hc32[n, pl.ds(i, 1)], pltpu.roll(out, 1, 0))
            under = jnp.where(last, hc32[2 + n, pl.ds(i, 1)], pltpu.roll(out, 7, 0))
            b = 2 * n
            sides.append(own + (weights[0][b] * over + weights[1][b] * out + weights[2][b] * under))
        sendb[tile * 2 + 1, frame] = jnp.concatenate(sides, 0).astype(BF16)
        sendb[(4 + tile) * 2 + 1, frame] = jnp.concatenate(ends, 0).astype(BF16)
        return carry

    lax.fori_loop(0, 16, border, 0)
    spread(1, 0)
    spread(1, 1)

    loads[2].wait()
    loads[3].wait()
    kf[...] = kt[...].astype(F32)
    kb[0:8] = jnp.zeros((8, 8, 128), F32)

    def widen(lag, carry):
        kb[8 + lag] = jnp.broadcast_to(kf[pl.ds(lag, 1)], (8, 128))
        return carry

    lax.fori_loop(0, 64, widen, 0)
    kb[8] = kb[8] + jnp.broadcast_to(sk[...], (8, 128))
    loads[4].wait()
    raw = jnp.dot(xl[...].reshape(256, 512), wgv[...], preferred_element_type=F32)
    gate[...] = raw / (1.0 + jnp.exp(-raw))
    loads[5].wait()

    def filtered(src):
        copy = pltpu.make_async_remote_copy(
            src_ref=sendb.at[src], dst_ref=xin.at[src], send_sem=fs.at[src], recv_sem=fr.at[src],
            device_id=peer(src), device_id_type=MESH,
        )
        pl.when(src == me)(lambda: keep().wait())
        pl.when(src != me)(copy.wait_recv)

    def back(dest):
        return pltpu.make_async_remote_copy(
            src_ref=retb.at[dest], dst_ref=mixin.at[me], send_sem=rs.at[dest], recv_sem=rr.at[me],
            device_id=peer(dest), device_id_type=MESH,
        )

    def own():
        return pltpu.make_async_copy(retb.at[me], mixin.at[me], rr.at[me])

    turn = lax.rem(ring + 4, 6)
    for turn_no, chip in enumerate([0, 1] + [2 + lax.rem(turn + step, 6) for step in (2, 4, 3, 1, 5, 0)]):
        if turn_no in (0, 2):
            for src in range(4) if turn_no == 0 else range(4, 16):
                filtered(src)

        def lagged(source, acc):
            shift = 8 + 8 * (chip - source)
            for s in range(8):
                x = xin[source * 2 + s // 4, s % 4].astype(F32).reshape(1, 2, 8, 128)
                acc = acc + kb[pl.ds(shift - s, 8)].reshape(8, 1, 8, 128) * x
            return acc

        acc = lax.fori_loop(0, chip + 1, lagged, jnp.zeros((8, 2, 8, 128), F32))
        retb[pl.ds(chip * 2, 2)] = acc.reshape(2, 4, 16, 128).astype(BF16)
        for dest in (chip * 2, chip * 2 + 1):
            pl.when(dest == me)(lambda: own().start())
            pl.when(dest != me)(back(dest).start)

    def arrived(which):
        for step in ORDER:
            src = lax.rem(ring + step, 8) * 2 + which

            def wait():
                pltpu.make_async_remote_copy(
                    src_ref=retb.at[src], dst_ref=mixin.at[src], send_sem=rs.at[src], recv_sem=rr.at[src],
                    device_id=peer(src), device_id_type=MESH,
                ).wait_recv()

            if step:
                wait()
            else:
                pl.when(core == which)(lambda: own().wait())
                pl.when(core != which)(wait)

    def values(which):
        rows = []
        for group in (2 * which, 2 * which + 1):
            rows.append(jnp.concatenate([mixin[owner(group, t)].reshape(64, 128) for t in range(4)], 1))
        return jnp.dot(jnp.concatenate(rows, 0), wvv[...], preferred_element_type=F32)

    def part(block, group, tile, frame, half):
        at = group * 64 + frame * 16 + half * 8
        return block[at : at + 8, tile * 128 : tile * 128 + 128]

    arrived(0)
    v = values(0)
    for tile in range(4):
        for frame in range(4):
            base = (tile * 4 + frame) * 64
            one, two = part(v, 0, tile, frame, 0), part(v, 0, tile, frame, 1)
            three, four = part(v, 1, tile, frame, 0), part(v, 1, tile, frame, 1)
            s1[base + 8 : base + 16] = one
            s1[base + 16 : base + 24] = two
            s1[base + 24 : base + 32] = three
            s1[base + 32 : base + 40] = four
            s1[base + 40 : base + 48] = jnp.where(
                sub < 3, pltpu.roll(one, 2, 0), jnp.where(sub < 5, pltpu.roll(two, 4, 0), pltpu.roll(three, 6, 0))
            )
            s1[base + 48 : base + 56] = pltpu.roll(four, 2, 0)
    arrived(1)
    v = values(1)
    for tile in range(4):
        for frame in range(4):
            base = (tile * 4 + frame) * 64
            top, bottom = part(v, 1, tile, frame, 0), part(v, 1, tile, frame, 1)
            s1[base : base + 8] = top
            s1[base + 56 : base + 64] = bottom
            s1[base + 48 : base + 56] = jnp.where(
                sub < 3, s1[base + 48 : base + 56], jnp.where(sub < 5, pltpu.roll(top, 4, 0), pltpu.roll(bottom, 6, 0))
            )
            s1[pl.ds(base, 8, stride=8)] = part(v, 0, tile, frame, 0)
            s1[pl.ds(base + 7, 8, stride=8)] = part(v, 0, tile, frame, 1)
            rows, chans = slice(frame * 64, frame * 64 + 64), slice(tile * 128, tile * 128 + 128)
            hid[rows, chans] = (s1[base : base + 64] * gate[rows, chans]).astype(BF16)

    for copy, has in zip(halo, there):
        pl.when(has)(copy.wait_send)
    for step in range(1, 16):
        dest = lax.rem(me + step, 16)
        forward(dest).wait_send()
        back(dest).wait_send()


def body(latents, spatial_taps, kernel_taps, skip_gain, gate_weight, value_weight, out_weight):
    dma = pltpu.SemaphoreType.DMA
    hidden = pl.pallas_call(
        kernel,
        out_shape=pltpu.VMEM((256, 512), BF16),
        in_specs=[pl.BlockSpec(memory_space=pl.ANY)] * 6,
        out_specs=pl.BlockSpec(memory_space=pltpu.VMEM),
        scratch_shapes=[
            pltpu.VMEM((4, 8, 8, 512), BF16),
            pltpu.VMEM((3, 3, 512), F32),
            pltpu.VMEM((64, 128), BF16),
            pltpu.VMEM((64, 128), F32),
            pltpu.VMEM((72, 8, 128), F32),
            pltpu.VMEM((1, 128), F32),
            pltpu.VMEM((512, 512), BF16),
            pltpu.VMEM((512, 512), BF16),
            pltpu.VMEM((1024, 128), F32),
            pltpu.VMEM((1024, 128), F32),
            pltpu.VMEM((2, 128, 128), BF16),
            pltpu.VMEM((4, 16, 128), BF16),
            pltpu.VMEM((2, 4, 8, 512), BF16),
            pltpu.VMEM((2, 128, 128), BF16),
            pltpu.VMEM((4, 16, 128), BF16),
            pltpu.VMEM((4, 16, 128), F32),
            pltpu.VMEM((2, 128, 128), F32),
            pltpu.VMEM((16, 4, 16, 128), BF16),
            pltpu.VMEM((16, 4, 16, 128), BF16),
            pltpu.VMEM((16, 4, 16, 128), BF16),
            pltpu.VMEM((16, 4, 16, 128), BF16),
            pltpu.VMEM((256, 512), F32),
            dma((6,)), dma((8,)), dma((8,)), dma((16,)), dma((16,)), dma((16,)), dma((16,)),
        ],
        compiler_params=pltpu.CompilerParams(
            collective_id=0, has_side_effects=True, vmem_limit_bytes=60 * 1024 * 1024
        ),
        name="mixing",
    )(latents, spatial_taps, kernel_taps, skip_gain.reshape(1, -1), gate_weight, value_weight)
    result = jnp.dot(hidden, out_weight, preferred_element_type=F32).astype(BF16)
    return result.reshape(latents.shape)


def solution(mesh):
    in_specs = (P("tm", "height", "width", None), P(), P(), P(), P(), P(), P())
    out_specs = P("tm", "height", "width", None)
    return jax.shard_map(body, mesh=mesh, in_specs=in_specs, out_specs=out_specs, check_vma=False)
```
